32 devices in a mesh: groups: 2 (over x), tensor: 8 (over z, y), pool: 2 (over core).
Axes of the slice: x: 2, y: 2, z: 4, core: 2. Of those that a mesh axis runs over, the one named last changes fastest.
Arguments:
- inputs: bfloat16 [2, 256, 8192], P(None, ('groups', 'pool')), parts along dimension 1, may hold values from -6 to 6
- query_weight: bfloat16 [8192, 8192], P(None, 'tensor'), may hold values from -0.0625 to 0.0625
- key_value_weight: bfloat16 [8192, 1024], P(None, 'tensor'), may hold values from -0.0625 to 0.0625
- key_value_cache: bfloat16 [256, 8, 2, 128, 128], P(('groups', 'pool'), 'tensor'), parts along dimension 0, may hold values from -330 to 330
- lengths: int32 [256], P(('groups', 'pool')), parts along dimension 0, may hold values from 1 to 256, as said below
- request_adapter: int32 [256], P(('groups', 'pool')), parts along dimension 0, may hold values from 0 to 255, as said below
- adapter_storage_row: int32 [512], P('groups'), parts along dimension 0, may hold values from 0 to 255, as said below
- adapter_down_factors: bfloat16 [512, 64, 8192], P(('groups', 'tensor', 'pool')), parts along dimension 0, may hold values from -0.0625 to 0.0625
- adapter_up_factors: bfloat16 [512, 64, 8192], P(('groups', 'tensor', 'pool')), parts along dimension 0, may hold values from -0.75 to 0.75
Outputs:
- attended: bfloat16 [2, 256, 8192], P(None, ('groups', 'pool'), 'tensor'), parts along dimension 1
The draws below stay inside these ranges and needn't reach their ends.
There are 2 independent parts, one for each index of `groups`. The reference program is written for one: setup_inputs(seed, part) draws one part's arguments, and reference() takes and returns one part's arrays. A program takes and returns all parts, laid end to end along the dimension named above; an argument that names none is the same for every part. Nothing has to cross between parts.
Inputs may be any that keep to these rules, and one draw needn't show every extreme that they name: `adapter_storage_row`: storage row r lies on device r // 16 of tensor and pool taken together, tensor index major; every row appears once. `request_adapter`: among the 64 requests of one pool index, at most 8 use adapters stored on the same device; in every group one device holds the adapters of exactly 8 requests of every pool index. `lengths`: every pool index has a request of length 256.
All inputs are finite; a program needn't handle non-finite values.
Results may differ from the reference program's by a relative error of at most 0.012.
Values may be sent and summed in bfloat16 or wider, within the bound.
No kernel may reach another device: no remote copies, remote signals or barrier semaphores. Data moves between devices by JAX's collectives and lax.ppermute only.
A program may use at most 320 MiB of HBM per device.

```python
import jax
import jax.numpy as jnp
from jax import lax

MODEL_DIMENSION = 8192
QUERY_HEADS = 64
HEAD_SIZE = 128
ADAPTER_RANK = 64
REQ_DEV = 64
CTX_PART = 128
KV_HEADS = 4
QUERY_FEATURES = 8192
SPLIT = 2
CTX = 256
OWNERS = 16
CAP = 8
ADP_DEV = 16
ADAPTER_POOL = 256
REQUEST_GROUP = 128
N_TENSOR = 8


def shared_draw(key):
    order = jax.random.permutation(jax.random.fold_in(key, 11), ADAPTER_POOL)
    inverse = jnp.argsort(order)
    slot_total = OWNERS * CAP
    favored = jax.random.randint(jax.random.fold_in(key, 12), (), 0, OWNERS)

    def one_block(block_key):
        shuffle = jax.random.permutation(jax.random.fold_in(block_key, 1), slot_total)
        owner_of_slot = jnp.arange(slot_total, dtype=jnp.int32) // CAP
        score = jnp.where(owner_of_slot == favored, shuffle - slot_total, shuffle)
        chosen = jnp.argsort(score)[:REQ_DEV]
        chosen = jax.random.permutation(jax.random.fold_in(block_key, 2), chosen)
        owner = chosen // CAP
        row = jax.random.randint(jax.random.fold_in(block_key, 3), (REQ_DEV,), 0, ADP_DEV)
        return inverse[owner * ADP_DEV + row]
    block_keys = jax.random.split(jax.random.fold_in(key, 13), REQUEST_GROUP // REQ_DEV)
    chosen_ids = jax.vmap(one_block)(block_keys).reshape(REQUEST_GROUP)
    return (order.astype(jnp.int32), chosen_ids.astype(jnp.int32))


def draw_adapter_storage_row(key, part):
    order, chosen_ids = shared_draw(key)
    return order


def draw_request_adapter(key, part):
    order, chosen_ids = shared_draw(key)
    return chosen_ids


def draw_lengths(key, part):
    key = jax.random.fold_in(key, 5)
    first = jax.random.randint(jax.random.fold_in(key, 1), (REQUEST_GROUP,), 1, CTX + 1)
    second = jax.random.randint(jax.random.fold_in(key, 2), (REQUEST_GROUP,), 1, CTX + 1)
    forced = jax.random.randint(jax.random.fold_in(key, 3), (REQUEST_GROUP // REQ_DEV,), 0, REQ_DEV)
    within = jnp.arange(REQUEST_GROUP, dtype=jnp.int32) % REQ_DEV
    block = jnp.arange(REQUEST_GROUP, dtype=jnp.int32) // REQ_DEV
    return jnp.where(within == forced[block], CTX, jnp.minimum(first, second)).astype(jnp.int32)


def draw_key_value_cache(key, part):
    key = jax.random.fold_in(key, 7)
    array_shape = (REQUEST_GROUP, N_TENSOR, 2, CTX_PART, HEAD_SIZE)
    value = jnp.clip(jax.random.normal(jax.random.fold_in(key, 1), array_shape, jnp.float32), -5.0, 5.0)
    return value.astype(jnp.bfloat16)


def block_levels(key, dims, cuts, low, high):
    gain = 1.0
    for axis_at, parts in cuts:
        steps = jax.random.uniform(jax.random.fold_in(jax.random.fold_in(key, 6), axis_at), (parts,), jnp.float32, low / len(cuts), high / len(cuts))
        gain = gain * jnp.repeat(jnp.exp(steps), dims[axis_at] // parts).reshape((-1,) + (1,) * (len(dims) - 1 - axis_at))
    return gain


def gaussian(stream_key, extent, width, bound, cuts=(), kind=jnp.bfloat16):
    level = block_levels(stream_key, extent, cuts, -0.22, 0.18) if cuts else 1.0
    result = jax.random.normal(stream_key, extent, jnp.float32) * width * level
    return jnp.minimum(jnp.maximum(result, -bound), bound).astype(kind)


def setup_inputs(seed: int = 0, part: int = 0) -> dict:
    key_of = jax.random.split(jax.random.key(seed), 10)
    part_keys = jax.random.split(jax.random.fold_in(key_of[9], part), 10)
    inputs = gaussian(part_keys[0], (2, REQUEST_GROUP, MODEL_DIMENSION), 1.0, 6.0, ((1, 2),))
    query_weight = gaussian(key_of[1], (MODEL_DIMENSION, QUERY_FEATURES), MODEL_DIMENSION ** -0.5, 0.0625, ((1, 8),))
    key_value_weight = gaussian(key_of[2], (MODEL_DIMENSION, 2 * KV_HEADS * HEAD_SIZE), MODEL_DIMENSION ** -0.5, 0.0625, ((1, 8),))
    key_value_cache = draw_key_value_cache(jax.random.fold_in(jax.random.fold_in(key_of[9], part), 71), part)
    lengths = draw_lengths(jax.random.fold_in(jax.random.fold_in(key_of[9], part), 71), part)
    request_adapter = draw_request_adapter(jax.random.fold_in(jax.random.fold_in(key_of[9], part), 71), part)
    adapter_storage_row = draw_adapter_storage_row(jax.random.fold_in(jax.random.fold_in(key_of[9], part), 71), part)
    adapter_down_factors = gaussian(part_keys[7], (ADAPTER_POOL, ADAPTER_RANK, MODEL_DIMENSION), MODEL_DIMENSION ** -0.5, 0.0625, ((0, 16),))
    adapter_up_factors = gaussian(part_keys[8], (ADAPTER_POOL, ADAPTER_RANK, QUERY_FEATURES), ADAPTER_RANK ** -0.5, 0.75, ((0, 16),))
    return dict(inputs=inputs, query_weight=query_weight, key_value_weight=key_value_weight, key_value_cache=key_value_cache, lengths=lengths, request_adapter=request_adapter, adapter_storage_row=adapter_storage_row, adapter_down_factors=adapter_down_factors, adapter_up_factors=adapter_up_factors)


ROPE_BASE = 500000.0
ADAPTER_SCALE = 0.5
MASKED = -1e30


def rotate(vector, position):
    half = vector.shape[-1] // 2
    freq = ROPE_BASE ** (-2.0 * jnp.arange(half, dtype=jnp.float32) / vector.shape[-1])
    angle = position.astype(jnp.float32)[..., None] * freq
    cosine = jnp.cos(angle)
    sine = jnp.sin(angle)
    first = vector[..., :half]
    second = vector[..., half:]
    return jnp.concatenate([first * cosine - second * sine, second * cosine + first * sine], axis=-1)


def to_half(value):
    return lax.optimization_barrier(value.astype(jnp.bfloat16)).astype(jnp.float32)


def reference(inputs, query_weight, key_value_weight, key_value_cache, lengths, request_adapter, adapter_storage_row, adapter_down_factors, adapter_up_factors):
    decode_step_count = inputs.shape[0]
    storage_rows = adapter_storage_row[request_adapter]
    selected_down = adapter_down_factors[storage_rows].astype(jnp.float32)
    selected_up = adapter_up_factors[storage_rows].astype(jnp.float32)
    flat = inputs.reshape(decode_step_count * REQUEST_GROUP, MODEL_DIMENSION)
    projected_rows = jnp.dot(flat, query_weight, preferred_element_type=jnp.float32).reshape(decode_step_count, REQUEST_GROUP, QUERY_FEATURES)
    reduced_rank_product = to_half(jnp.einsum('srd,rkd->srk', inputs.astype(jnp.float32), selected_down))
    adapter_correction = jnp.einsum('ybz,bzo->ybo', reduced_rank_product, selected_up)
    positions = lengths[None, :] + jnp.arange(decode_step_count, dtype=jnp.int32)[:, None]
    query_vectors = (projected_rows + ADAPTER_SCALE * adapter_correction).reshape(decode_step_count, REQUEST_GROUP, QUERY_HEADS, HEAD_SIZE)
    query_vectors = to_half(rotate(query_vectors, positions[:, :, None]))
    fresh_kv = jnp.dot(flat, key_value_weight, preferred_element_type=jnp.float32).reshape(decode_step_count, REQUEST_GROUP, KV_HEADS, 2, HEAD_SIZE)
    new_keys = to_half(rotate(fresh_kv[:, :, :, 0], positions[:, :, None]))
    new_vals = to_half(fresh_kv[:, :, :, 1])
    cache = key_value_cache.astype(jnp.float32).reshape(REQUEST_GROUP, KV_HEADS, SPLIT, 2, CTX_PART, HEAD_SIZE)
    cached_keys = cache[:, :, :, 0].reshape(REQUEST_GROUP, KV_HEADS, CTX, HEAD_SIZE)
    cached_vals = cache[:, :, :, 1].reshape(REQUEST_GROUP, KV_HEADS, CTX, HEAD_SIZE)
    grouped = query_vectors.reshape(decode_step_count, REQUEST_GROUP, KV_HEADS, QUERY_HEADS // KV_HEADS, HEAD_SIZE)
    scale = HEAD_SIZE ** -0.5
    cached = jnp.einsum('srhgd,rhjd->srhgj', grouped, cached_keys) * scale
    valid = jnp.arange(CTX, dtype=jnp.int32)[None, :] < lengths[:, None]
    cached = jnp.where(valid[None, :, None, None, :], cached, MASKED)
    recent = jnp.einsum('srhgd,irhd->srhgi', grouped, new_keys) * scale
    order_ok = jnp.arange(decode_step_count)[None, :] <= jnp.arange(decode_step_count)[:, None]
    recent = jnp.where(order_ok[:, None, None, None, :], recent, MASKED)
    top = jnp.maximum(jnp.max(cached, axis=-1, keepdims=True), jnp.max(recent, axis=-1, keepdims=True))
    e_cached = jnp.exp(cached - top)
    e_recent = jnp.exp(recent - top)
    total = jnp.sum(e_cached, axis=-1, keepdims=True) + jnp.sum(e_recent, axis=-1, keepdims=True)
    acc = jnp.einsum('srhgj,rhjd->srhgd', to_half(e_cached), cached_vals)
    acc = acc + jnp.einsum('srhgi,irhd->srhgd', to_half(e_recent), new_vals)
    return (acc / total).astype(jnp.bfloat16).reshape(decode_step_count, REQUEST_GROUP, QUERY_FEATURES)
```

```python
import functools

import jax
import jax.numpy as jnp
import numpy as np
from jax import lax
from jax.experimental import pallas as pl
from jax.experimental.pallas import tpu as pltpu
from jax.sharding import PartitionSpec as P

ROPE_BASE = 500000.0
ADAPTER_SCALE = 0.5
MASKED = -1e30
BF = jnp.bfloat16
F32 = jnp.float32
I32 = jnp.int32


def swapped(value, axis, bit):
    mask = 2**bit
    pairs = [(source, source ^ mask) for source in range(lax.axis_size(axis))]
    return lax.ppermute(value, axis, pairs)


def iota(shape, axis):
    return lax.broadcasted_iota(I32, shape, axis)


def column_of(row):
    count = row.shape[1]
    eye = iota((count, count), 0) == iota((count, count), 1)
    return jnp.sum(jnp.where(eye, row, jnp.zeros_like(row)), axis=1, keepdims=True)


def row_of(column):
    count = column.shape[0]
    eye = iota((count, count), 0) == iota((count, count), 1)
    return jnp.sum(jnp.where(eye, column, jnp.zeros_like(column)), axis=0, keepdims=True)


def routes(adapters, table, per_owner):
    requests = adapters.shape[1]
    rows = table.shape[1]
    match = (iota((rows, requests), 0) == adapters).astype(F32)
    stored = jnp.dot(
        table.astype(F32), match, precision=lax.Precision.HIGHEST, preferred_element_type=F32
    ).astype(I32)
    owner = stored // per_owner
    local_row = stored - owner * per_owner
    owner_column = column_of(owner)
    ahead = iota((requests, requests), 0) < iota((requests, requests), 1)
    place = jnp.sum(
        jnp.where((owner_column == owner) & ahead, 1, 0), axis=0, keepdims=True
    )
    return owner, local_row, place


def stage_kernel(states_hbm, down_hbm, adapters_hbm, table_hbm, *rest):
    states, down, adapters, table, sem, other_sem = rest
    parts = sem.shape[0]
    size = down.shape[0] // parts
    copies = [
        pltpu.make_async_copy(states_hbm, states, other_sem.at[0]),
        pltpu.make_async_copy(adapters_hbm, adapters, other_sem.at[1]),
        pltpu.make_async_copy(table_hbm, table, other_sem.at[2]),
    ]
    for part in range(parts):
        span = pl.ds(part * size, size)
        copies.append(pltpu.make_async_copy(down_hbm.at[span], down.at[span], sem.at[part]))
    for copy in copies:
        copy.start()
    for copy in copies:
        copy.wait()


def lora_kernel(
    dims,
    own_ref,
    other_ref,
    own_adapters_ref,
    other_adapters_ref,
    table_ref,
    down,
    down_hbm,
    up_hbm,
    out_ref,
    down_rest,
    up,
    chosen,
    low,
    down_sem,
    up_sem,
):
    steps, requests, capacity, per_owner, rank, tensor_count, pool_count = dims
    here_rows = down.shape[0]
    down_rows = down_rest.shape[0]
    up_parts = up_sem.shape[0]
    up_columns = up.shape[1] // up_parts
    rest_copy = pltpu.make_async_copy(
        down_hbm.at[pl.ds(here_rows, down_rows)], down_rest, down_sem.at[0]
    )

    def up_copy(part):
        columns = pl.ds(pl.multiple_of(part * up_columns, up_columns), up_columns)
        return pltpu.make_async_copy(
            up_hbm.at[:, columns], up.at[:, columns], up_sem.at[part]
        )

    rest_copy.start()

    @pl.loop(0, up_parts)
    def _(part):
        up_copy(part).start()

    pool = lax.axis_index("pool")
    me = lax.axis_index("tensor") * pool_count + pool
    table = table_ref[...]
    rows = steps * capacity
    local_rows = []
    for which, (states_ref, adapters_ref) in enumerate(
        ((own_ref, own_adapters_ref), (other_ref, other_adapters_ref))
    ):
        owner, local_row, place = routes(adapters_ref[...], table, per_owner)
        owner = jnp.concatenate([owner] * steps, axis=1)
        place = jnp.concatenate([place] * steps, axis=1)
        local_row = jnp.concatenate([local_row] * steps, axis=1)
        shape = (rows, steps * requests)
        row = iota(shape, 0)
        row_step = row // capacity
        hit = (
            (owner == me)
            & (place == row - row_step * capacity)
            & (row_step == iota(shape, 1) // requests)
        )
        local_rows.append(jnp.sum(jnp.where(hit, local_row, 0), axis=1, keepdims=True))
        pick = jnp.where(hit, 1.0, 0.0).astype(BF)
        chosen[which] = jnp.dot(
            pick, states_ref[...], preferred_element_type=F32
        ).astype(BF)
    local_rows = jnp.concatenate(local_rows, axis=0)
    states = jnp.concatenate([chosen[0], chosen[1]], axis=0)

    def factors_of(rows_ref, first_row):
        count = rows_ref.shape[0]
        piece = lax.dot_general(
            rows_ref[...], states, (((1,), (1,)), ((), ())), preferred_element_type=F32
        ).T
        holder = (iota(piece.shape, 1) + first_row) // rank
        low[:, pl.ds(first_row, count)] = jnp.where(
            holder == local_rows, piece.astype(BF), jnp.zeros(piece.shape, BF)
        )

    for first_row in range(0, here_rows, down_rows):
        factors_of(down.at[pl.ds(first_row, down_rows)], first_row)

    @pl.loop(0, 1)
    def _(_):
        rest_copy.wait()

    factors_of(down_rest, here_rows)

    @pl.loop(0, up_parts)
    def _(part):
        up_copy(part).wait()
        columns = pl.ds(pl.multiple_of(part * up_columns, up_columns), up_columns)
        term = jnp.dot(low[...], up[:, columns], preferred_element_type=F32).astype(BF)
        out_ref[part * pool_count + pool] = term[:rows]
        out_ref[part * pool_count + 1 - pool] = term[rows:]


def project_kernel(
    dims,
    states_ref,
    adapters_ref,
    table_ref,
    lengths_ref,
    freq_ref,
    weight_hbm,
    new_weight_hbm,
    out_ref,
    piece_ref,
    cosine_ref,
    sine_ref,
    spread_ref,
    weight,
    new_weight,
    sem,
):
    steps, requests, capacity, per_owner = dims
    parts = sem.shape[0] - 1
    depth = weight.shape[0] // parts
    new_copy = pltpu.make_async_copy(new_weight_hbm, new_weight, sem.at[parts])

    def part_copy(part):
        span = pl.ds(pl.multiple_of(part * depth, depth), depth)
        return pltpu.make_async_copy(weight_hbm.at[span], weight.at[span], sem.at[part])

    @pl.loop(0, parts)
    def _(part):
        part_copy(part).start()

    new_copy.start()

    rows = steps * capacity
    owner, _, place = routes(adapters_ref[...], table_ref[...], per_owner)
    owner = jnp.concatenate([column_of(owner)] * steps, axis=0)
    place = jnp.concatenate([column_of(place)] * steps, axis=0)
    shape = spread_ref.shape
    slot = iota(shape, 1)
    slot_owner = slot // rows
    slot_step = (slot - slot_owner * rows) // capacity
    slot_place = slot - slot_owner * rows - slot_step * capacity
    hit = (
        (slot_owner == owner)
        & (slot_place == place)
        & (slot_step == iota(shape, 0) // requests)
    )
    spread_ref[...] = jnp.where(hit, 1.0, 0.0).astype(BF)

    length = column_of(lengths_ref[...])
    position = jnp.concatenate([length + step for step in range(steps)], axis=0)
    angle = position.astype(F32) * freq_ref[...]
    cosine = jnp.cos(angle)
    sine = jnp.sin(angle)
    half = angle.shape[1] // 2
    sine = jnp.where(iota(angle.shape, 1) < half, -sine, sine)
    cosine_ref[...] = cosine
    sine_ref[...] = sine

    out_ref[...] = jnp.zeros_like(out_ref)

    @pl.loop(0, parts)
    def _(part):
        part_copy(part).wait()
        span = pl.ds(pl.multiple_of(part * depth, depth), depth)
        out_ref[...] += jnp.dot(
            states_ref[:, span], weight[span, :], preferred_element_type=F32
        )

    new_copy.wait()
    fresh = jnp.dot(states_ref[...], new_weight[...], preferred_element_type=F32)
    turned = fresh * cosine_ref[...] + pltpu.roll(fresh, half, 1) * sine_ref[...]
    is_first = lax.axis_index("tensor") % 2 == 0
    piece_ref[...] = jnp.where(is_first, turned, fresh).astype(BF)


def load_kernel(source, after, out_ref, sem):
    copy = pltpu.make_async_copy(source, out_ref, sem.at[0])
    copy.start()
    copy.wait()


def query_kernel(
    dims, terms_ref, spread_ref, projected_ref, piece_ref, cosine_ref, sine_ref, out_ref, packed
):
    steps, requests, heads, head_width = dims
    correction = jnp.dot(spread_ref[...], terms_ref[...], preferred_element_type=F32)
    query = projected_ref[...] + ADAPTER_SCALE * correction
    cosine = cosine_ref[...]
    sine = sine_ref[...]
    count = packed.shape[0]
    for head in range(heads):
        vector = query[:, head * head_width : (head + 1) * head_width]
        vector = vector * cosine + pltpu.roll(vector, head_width // 2, 1) * sine
        for step in range(steps):
            packed[pl.ds(step * heads + head, requests, stride=steps * heads), :] = vector[
                step * requests : (step + 1) * requests
            ]
    out_ref[:count, :] = packed[...].astype(BF)
    out_ref[count:, :] = piece_ref[...]


def attend(dims, lengths_ref, query_ref, cache_ref, keys, vals, scratch, store):
    steps, requests, heads, head_width, kv_split = dims
    scores_ref, recent_ref, weights_ref, new_weights_ref, acc_ref = scratch
    per_request = steps * heads
    count = requests * per_request
    scale = head_width ** (-0.5)
    context = cache_ref.shape[2]
    part = lax.axis_index("tensor") % kv_split
    base = part * context
    lane = iota((per_request, context), 1)
    for request in range(requests):
        span = pl.ds(request * per_request, per_request)
        score = lax.dot_general(
            query_ref[span, :],
            cache_ref[request, 0],
            (((1,), (1,)), ((), ())),
            preferred_element_type=F32,
        )
        scores_ref[span, :] = jnp.where(
            lane < lengths_ref[request] - base, score * scale, MASKED
        )
    rows = min(128, count)
    shape = (rows, steps * requests)
    column_step = iota(shape, 1) // requests
    column_request = iota(shape, 1) - column_step * requests
    row_request = iota(shape, 0) // per_request
    row_step = (iota(shape, 0) - row_request * per_request) // heads
    allowed = (column_step <= row_step) & (part == 0)
    ahead = column_request - row_request
    for at in range(count // rows):
        span = pl.ds(at * rows, rows)
        recent = lax.dot_general(
            query_ref[span, :], keys, (((1,), (1,)), ((), ())), preferred_element_type=F32
        )
        recent_ref[span, :] = jnp.where(
            allowed & (ahead == at * (rows // per_request)), recent * scale, MASKED
        )
    totals = []
    for at in range(count // rows):
        span = pl.ds(at * rows, rows)
        scores = scores_ref[span, :]
        recent = recent_ref[span, :]
        top = jnp.maximum(
            jnp.max(scores, axis=1, keepdims=True), jnp.max(recent, axis=1, keepdims=True)
        ) if scores.shape != recent.shape else jnp.max(
            jnp.maximum(scores, recent), axis=1, keepdims=True
        )
        e_cached = jnp.exp(scores - top)
        e_recent = jnp.exp(recent - top)
        total = (
            jnp.sum(e_cached, axis=1, keepdims=True) + jnp.sum(e_recent, axis=1, keepdims=True)
            if scores.shape != recent.shape
            else jnp.sum(e_cached + e_recent, axis=1, keepdims=True)
        )
        weights_ref[span, :] = e_cached.astype(BF)
        new_weights_ref[span, :] = e_recent.astype(BF)
        totals.append((top, total))
    for request in range(requests):
        span = pl.ds(request * per_request, per_request)
        acc_ref[span, :] = jnp.dot(
            weights_ref[span, :], cache_ref[request, 1], preferred_element_type=F32
        )
    for at in range(count // rows):
        span = pl.ds(at * rows, rows)
        top, total = totals[at]
        acc = acc_ref[span, :] + jnp.dot(
            new_weights_ref[span, :], vals, preferred_element_type=F32
        )
        store(at, rows, acc * (1.0 / total), top + jnp.log(total))


def new_pieces(own, other):
    first = lax.axis_index("tensor") % 2 == 0
    keys = jnp.where(first, own.astype(F32), other.astype(F32)).astype(BF)
    vals = jnp.where(first, other.astype(F32), own.astype(F32)).astype(BF)
    return keys, vals


def own_kernel(dims, lengths_ref, sent_ref, got_ref, cache_ref, out_ref, level_ref, *scratch):
    count = out_ref.shape[0]
    keys, vals = new_pieces(sent_ref[count:, :], got_ref[count:, :])

    def store(at, rows, result, level):
        out_ref[pl.ds(at * rows, rows), :] = result
        level_ref[pl.ds(at * rows, rows), :] = level

    attend(dims, lengths_ref, sent_ref, cache_ref, keys, vals, scratch, store)


def send_kernel(dims, lengths_ref, sent_ref, got_ref, cache_ref, out_ref, levels, *scratch):
    lines = levels.shape[0]
    count = lines * 128
    keys, vals = new_pieces(sent_ref[count:, :], got_ref[count:, :])

    def store(at, rows, result, level):
        out_ref[pl.ds(at * rows, rows), :] = result.astype(BF)
        for line in range(rows // 128):
            levels[pl.ds(at * (rows // 128) + line, 1), :] = row_of(
                level[line * 128 : (line + 1) * 128]
            )

    attend(dims, lengths_ref, got_ref, cache_ref, keys, vals, scratch, store)
    rest = levels[...]
    pieces = []
    for _ in range(3):
        piece = rest.astype(BF)
        pieces.append(piece)
        rest = rest - piece.astype(F32)
    pieces.append(jnp.zeros_like(pieces[0]))
    out_ref[pl.ds(count, 4 * lines), :] = jnp.concatenate(pieces, axis=0)


def merge_kernel(dims, own_ref, level_ref, got_ref, out_ref, packed):
    steps, requests, heads, head_width = dims
    count = own_ref.shape[0]
    lines = count // 128
    extra = got_ref[pl.ds(count, 4 * lines), :].astype(F32)
    other_level = extra[:lines] + extra[lines : 2 * lines] + extra[2 * lines : 3 * lines]
    for line in range(lines):
        span = pl.ds(line * 128, 128)
        theirs = column_of(other_level[line : line + 1])
        mine = level_ref[span, :]
        top = jnp.maximum(mine, theirs)
        mine = jnp.exp(mine - top)
        theirs = jnp.exp(theirs - top)
        total = mine + theirs
        packed[span, :] = own_ref[span, :] * (mine / total) + got_ref[span, :].astype(F32) * (
            theirs / total
        )
    for step in range(steps):
        for head in range(heads):
            out_ref[
                step * requests : (step + 1) * requests,
                head * head_width : (head + 1) * head_width,
            ] = packed[pl.ds(step * heads + head, requests, stride=steps * heads), :].astype(BF)


def in_vmem(shape, dtype):
    return pltpu.VMEM(shape, dtype)


def in_hbm(value):
    return pltpu.with_memory_space_constraint(value, pltpu.HBM)


def vmem_limit(mebibytes):
    return pltpu.CompilerParams(vmem_limit_bytes=mebibytes * 2**20)


def whole(*refs):
    return [pl.BlockSpec(memory_space=pltpu.VMEM)] * len(refs)


def local(
    inputs,
    query_weight,
    key_value_weight,
    key_value_cache,
    lengths,
    request_adapter,
    adapter_storage_row,
    adapter_down_factors,
    adapter_up_factors,
):
    steps, requests, width = inputs.shape
    tensor_count = lax.axis_size("tensor")
    pool_count = lax.axis_size("pool")
    owners = tensor_count * pool_count
    head_width = key_value_cache.shape[-1]
    context = key_value_cache.shape[-2]
    kv_split = 2 * head_width // key_value_weight.shape[1]
    query_columns = query_weight.shape[1]
    heads = query_columns // head_width
    per_owner, rank, _ = adapter_down_factors.shape
    capacity = max(2, 2 * requests // owners)
    rows = steps * capacity
    count = steps * requests

    flat = inputs.reshape(count, width)
    adapters = request_adapter.reshape(1, requests)
    other_adapters = swapped(adapters, "pool", 0)
    other_flat = swapped(flat, "pool", 0)
    table = adapter_storage_row.reshape(1, -1)
    down = adapter_down_factors.reshape(per_owner * rank, width)
    up = adapter_up_factors.reshape(per_owner * rank, -1)
    cache = key_value_cache.reshape(requests, 2, context, head_width)
    anywhere = pl.BlockSpec(memory_space=pltpu.HBM)
    smem = pl.BlockSpec(memory_space=pltpu.SMEM)

    rest_rows = per_owner * rank // 4
    here_rows = per_owner * rank - rest_rows
    flat_here, down_here, adapters, table = pl.pallas_call(
        stage_kernel,
        out_shape=[
            in_vmem(flat.shape, BF),
            in_vmem((here_rows, width), BF),
            in_vmem(adapters.shape, I32),
            in_vmem(table.shape, I32),
        ],
        in_specs=[anywhere] * 4,
        out_specs=whole(*range(4)),
        scratch_shapes=[pltpu.SemaphoreType.DMA((3,)), pltpu.SemaphoreType.DMA((3,))],
        compiler_params=vmem_limit(4),
        cost_estimate=pl.CostEstimate(
            flops=0, bytes_accessed=2 * (down.size + flat.size), transcendentals=0
        ),
        name="stage",
    )(in_hbm(flat), in_hbm(down), in_hbm(adapters), in_hbm(table))

    lora_dims = (steps, requests, capacity, per_owner, rank, tensor_count, pool_count)
    outgoing = pl.pallas_call(
        functools.partial(lora_kernel, lora_dims),
        out_shape=jax.ShapeDtypeStruct((owners, rows, query_columns), BF),
        in_specs=whole(*range(6)) + [anywhere] * 2,
        out_specs=whole(0)[0],
        scratch_shapes=[
            pltpu.VMEM((rest_rows, width), BF),
            pltpu.VMEM(up.shape, BF),
            pltpu.VMEM((2, rows, width), BF),
            pltpu.VMEM((2 * rows, per_owner * rank), BF),
            pltpu.SemaphoreType.DMA((1,)),
            pltpu.SemaphoreType.DMA((tensor_count,)),
        ],
        compiler_params=vmem_limit(24),
        cost_estimate=pl.CostEstimate(
            flops=8 * rows * per_owner * rank * width,
            bytes_accessed=2 * per_owner * rank * width,
            transcendentals=0,
        ),
        name="lora",
    )(
        flat_here,
        pltpu.with_memory_space_constraint(other_flat, pltpu.VMEM),
        adapters,
        other_adapters,
        table,
        down_here,
        in_hbm(down),
        in_hbm(up),
    )
    terms = lax.all_to_all(outgoing, ("tensor", "pool"), split_axis=0, concat_axis=0, tiled=True)
    terms = terms.reshape(owners * rows, query_columns)

    flat_late, adapters, table, _ = lax.optimization_barrier(
        (flat_here, adapters, table, outgoing)
    )
    power = np.arange(head_width // 2, dtype=np.float64) * (-2.0 / head_width)
    freq = np.tile(ROPE_BASE**power, 2).astype(np.float32).reshape(1, head_width)
    projected, own_piece, cosine, sine, spread = pl.pallas_call(
        functools.partial(project_kernel, (steps, requests, capacity, per_owner)),
        out_shape=[
            in_vmem((count, query_columns), F32),
            in_vmem((count, head_width), BF),
            in_vmem((count, head_width), F32),
            in_vmem((count, head_width), F32),
            in_vmem((count, owners * rows), BF),
        ],
        in_specs=whole(*range(5)) + [anywhere] * 2,
        out_specs=whole(*range(5)),
        scratch_shapes=[
            pltpu.VMEM(query_weight.shape, BF),
            pltpu.VMEM(key_value_weight.shape, BF),
            pltpu.SemaphoreType.DMA((17,)),
        ],
        compiler_params=vmem_limit(24),
        cost_estimate=pl.CostEstimate(
            flops=2 * count * width * query_columns,
            bytes_accessed=2 * width * query_columns,
            transcendentals=0,
        ),
        name="project",
    )(
        flat_late,
        adapters,
        table,
        lengths.reshape(1, requests),
        jnp.asarray(freq),
        in_hbm(query_weight),
        in_hbm(key_value_weight),
    )

    dims = (steps, requests, heads, head_width)
    packed_rows = count * heads
    sent = pl.pallas_call(
        functools.partial(query_kernel, dims),
        out_shape=jax.ShapeDtypeStruct((packed_rows + count, head_width), BF),
        in_specs=whole(*range(6)),
        out_specs=whole(0)[0],
        scratch_shapes=[pltpu.VMEM((packed_rows, head_width), F32)],
        compiler_params=vmem_limit(8),
        name="query",
    )(terms, spread, projected, own_piece, cosine, sine)
    got = swapped(sent, "tensor", 0)

    cache_here = pl.pallas_call(
        load_kernel,
        out_shape=in_vmem(cache.shape, BF),
        in_specs=[anywhere, pl.BlockSpec(memory_space=pl.ANY)],
        out_specs=whole(0)[0],
        scratch_shapes=[pltpu.SemaphoreType.DMA((1,))],
        compiler_params=vmem_limit(1),
        cost_estimate=pl.CostEstimate(
            flops=0, bytes_accessed=4 * cache.size, transcendentals=0
        ),
        name="load",
    )(in_hbm(cache), sent)

    lines = packed_rows // 128
    attend_dims = (steps, requests, heads, head_width, kv_split)
    attend_scratch = [
        pltpu.VMEM((packed_rows, context), F32),
        pltpu.VMEM((packed_rows, count), F32),
        pltpu.VMEM((packed_rows, context), BF),
        pltpu.VMEM((packed_rows, count), BF),
        pltpu.VMEM((packed_rows, head_width), F32),
    ]
    cost = pl.CostEstimate(
        flops=4 * packed_rows * context * head_width,
        bytes_accessed=2 * cache.size,
        transcendentals=packed_rows * context,
    )
    sending = pl.pallas_call(
        functools.partial(send_kernel, attend_dims),
        out_shape=jax.ShapeDtypeStruct((packed_rows + 4 * lines, head_width), BF),
        in_specs=[smem] + whole(*range(3)),
        out_specs=whole(0)[0],
        scratch_shapes=[pltpu.VMEM((lines, 128), F32)] + attend_scratch,
        compiler_params=vmem_limit(12),
        cost_estimate=cost,
        name="send",
    )(lengths, sent, got, cache_here)
    partial = swapped(sending, "tensor", 0)
    own, level = pl.pallas_call(
        functools.partial(own_kernel, attend_dims),
        out_shape=[
            jax.ShapeDtypeStruct((packed_rows, head_width), F32),
            jax.ShapeDtypeStruct((packed_rows, 1), F32),
        ],
        in_specs=[smem] + whole(*range(3)),
        out_specs=whole(*range(2)),
        scratch_shapes=attend_scratch,
        compiler_params=vmem_limit(12),
        cost_estimate=cost,
        name="own",
    )(lengths, sent, got, cache_here)
    attended = pl.pallas_call(
        functools.partial(merge_kernel, dims),
        out_shape=jax.ShapeDtypeStruct((count, query_columns), BF),
        in_specs=whole(*range(3)),
        out_specs=whole(0)[0],
        scratch_shapes=[pltpu.VMEM((packed_rows, head_width), F32)],
        compiler_params=vmem_limit(8),
        name="merge",
    )(own, level, partial)
    return attended.reshape(steps, requests, query_columns)


def solution(mesh):
    placed = (
        P(None, ("groups", "pool"), None),
        P(None, "tensor"),
        P(None, "tensor"),
        P(("groups", "pool"), "tensor", None, None, None),
        P(("groups", "pool")),
        P(("groups", "pool")),
        P("groups"),
        P(("groups", "tensor", "pool"), None, None),
        P(("groups", "tensor", "pool"), None, None),
    )
    return jax.shard_map(
        local,
        mesh=mesh,
        in_specs=placed,
        out_specs=P(None, ("groups", "pool"), "tensor"),
        check_vma=False,
    )
```

```python
import functools

import jax
import jax.numpy as jnp
import numpy as np
from jax import lax
from jax.experimental import pallas as pl
from jax.experimental.pallas import tpu as pltpu
from jax.sharding import PartitionSpec as P

ROPE_BASE = 500000.0
ADAPTER_SCALE = 0.5
MASKED = -1e30
BF = jnp.bfloat16
F32 = jnp.float32
I32 = jnp.int32


def swapped(value, axis, bit):
    mask = 2**bit
    pairs = [(source, source ^ mask) for source in range(lax.axis_size(axis))]
    return lax.ppermute(value, axis, pairs)


def iota(shape, axis):
    return lax.broadcasted_iota(I32, shape, axis)


def column_of(row):
    count = row.shape[1]
    eye = iota((count, count), 0) == iota((count, count), 1)
    return jnp.sum(jnp.where(eye, row, jnp.zeros_like(row)), axis=1, keepdims=True)


def row_of(column):
    count = column.shape[0]
    eye = iota((count, count), 0) == iota((count, count), 1)
    return jnp.sum(jnp.where(eye, column, jnp.zeros_like(column)), axis=0, keepdims=True)


def routes(adapters, table, per_owner):
    requests = adapters.shape[1]
    rows = table.shape[1]
    match = (iota((rows, requests), 0) == adapters).astype(F32)
    stored = jnp.dot(
        table.astype(F32), match, precision=lax.Precision.HIGHEST, preferred_element_type=F32
    ).astype(I32)
    owner = stored // per_owner
    local_row = stored - owner * per_owner
    owner_column = column_of(owner)
    ahead = iota((requests, requests), 0) < iota((requests, requests), 1)
    place = jnp.sum(
        jnp.where((owner_column == owner) & ahead, 1, 0), axis=0, keepdims=True
    )
    return owner, local_row, place


def picked(dims, pools, states_ref, adapters, table):
    steps, requests, capacity, per_owner, pool_count = dims
    owner, local_row, place = routes(adapters, table, per_owner)
    owner = jnp.concatenate([owner] * steps, axis=1)
    place = jnp.concatenate([place] * steps, axis=1)
    local_row = jnp.concatenate([local_row] * steps, axis=1)
    shape = (steps * capacity, steps * requests)
    row = iota(shape, 0)
    row_step = row // capacity
    slot = (place == row - row_step * capacity) & (row_step == iota(shape, 1) // requests)
    hits = [
        slot & (owner == lax.axis_index("tensor") * pool_count + pool) for pool in pools
    ]
    pick = jnp.concatenate([jnp.where(hit, 1.0, 0.0) for hit in hits], axis=0).astype(BF)
    states = jnp.dot(pick, states_ref[...], preferred_element_type=F32).astype(BF)
    rows = [jnp.sum(jnp.where(hit, local_row, 0), axis=1, keepdims=True) for hit in hits]
    return states, rows


def stage_kernel(dims, states_hbm, down_hbm, adapters_hbm, table_hbm, *rest):
    states, down, adapters, table, own, own_rows, other, other_rows, sem, other_sem = rest
    parts = sem.shape[0]
    size = down.shape[0] // parts
    first = [
        pltpu.make_async_copy(adapters_hbm, adapters, other_sem.at[1]),
        pltpu.make_async_copy(table_hbm, table, other_sem.at[2]),
        pltpu.make_async_copy(states_hbm, states, other_sem.at[0]),
    ]
    copies = []
    for part in range(parts):
        span = pl.ds(part * size, size)
        copies.append(pltpu.make_async_copy(down_hbm.at[span], down.at[span], sem.at[part]))
    for copy in first + copies:
        copy.start()
    for copy in first:
        copy.wait()
    pool = lax.axis_index("pool")
    chosen, rows = picked(dims, (pool, 1 - pool), states, adapters[...], table[...])
    count = own.shape[0]
    own[...] = chosen[:count]
    other[...] = chosen[count:]
    own_rows[...] = rows[0]
    other_rows[...] = rows[1]
    for copy in copies:
        copy.wait()


def more_kernel(first_row, down_hbm, after, down, sem):
    parts = sem.shape[0]
    size = down.shape[0] // parts
    copies = [
        pltpu.make_async_copy(
            down_hbm.at[pl.ds(first_row + part * size, size)],
            down.at[pl.ds(part * size, size)],
            sem.at[part],
        )
        for part in range(parts)
    ]
    for copy in copies:
        copy.start()
    for copy in copies:
        copy.wait()


def lora_kernel(
    dims,
    rank,
    own_ref,
    own_rows_ref,
    other_ref,
    other_rows_ref,
    down_first,
    down_second,
    down_hbm,
    up_hbm,
    out_ref,
    down_rest,
    up,
    low,
    down_sem,
    up_sem,
):
    steps, requests, capacity, per_owner, pool_count = dims
    rows = steps * capacity
    here_rows = down_first.shape[0] + down_second.shape[0]
    down_rows = down_rest.shape[0]
    up_parts = up_sem.shape[0]
    up_columns = up.shape[1] // up_parts
    rest_copy = pltpu.make_async_copy(
        down_hbm.at[pl.ds(here_rows, down_rows)], down_rest, down_sem.at[0]
    )

    def up_copy(part):
        columns = pl.ds(pl.multiple_of(part * up_columns, up_columns), up_columns)
        return pltpu.make_async_copy(
            up_hbm.at[:, columns], up.at[:, columns], up_sem.at[part]
        )

    rest_copy.start()

    @pl.loop(0, up_parts)
    def _(part):
        up_copy(part).start()

    pool = lax.axis_index("pool")
    local_rows = jnp.concatenate([own_rows_ref[...], other_rows_ref[...]], axis=0)
    states = jnp.concatenate([own_ref[...].astype(F32), other_ref[...].astype(F32)], axis=0).T.astype(BF)

    def factors_of(rows_ref, first_row):
        count = rows_ref.shape[0]
        piece = lax.dot_general(
            rows_ref[...], states, (((1,), (0,)), ((), ())), preferred_element_type=F32
        ).T
        holder = (iota(piece.shape, 1) + first_row) // rank
        low[:, pl.ds(first_row, count)] = jnp.where(
            holder == local_rows, piece.astype(BF), jnp.zeros(piece.shape, BF)
        )

    first_row = 0
    for staged in (down_first, down_second):
        for at in range(0, staged.shape[0], down_rows):
            factors_of(staged.at[pl.ds(at, down_rows)], first_row)
            first_row += down_rows

    @pl.loop(0, 1)
    def _(_):
        rest_copy.wait()

    factors_of(down_rest, here_rows)
    factors = low[...]
    for part in range(up_parts):
        up_copy(part).wait()
        columns = pl.ds(part * up_columns, up_columns)
        term = jnp.dot(factors, up[:, columns], preferred_element_type=F32).astype(BF)
        out_ref[part * pool_count + pool] = term[:rows]
        out_ref[part * pool_count + 1 - pool] = term[rows:]


def project_kernel(
    dims,
    states_ref,
    adapters_ref,
    table_ref,
    lengths_ref,
    freq_ref,
    weight_hbm,
    new_weight_hbm,
    out_ref,
    piece_ref,
    cosine_ref,
    sine_ref,
    spread_ref,
    weight,
    new_weight,
    sem,
):
    steps, requests, capacity, per_owner = dims
    parts = sem.shape[0] - 1
    depth = weight.shape[0] // parts
    new_copy = pltpu.make_async_copy(new_weight_hbm, new_weight, sem.at[parts])

    def part_copy(part):
        span = pl.ds(pl.multiple_of(part * depth, depth), depth)
        return pltpu.make_async_copy(weight_hbm.at[span], weight.at[span], sem.at[part])

    @pl.loop(0, parts)
    def _(part):
        part_copy(part).start()

    new_copy.start()

    rows = steps * capacity
    owner, _, place = routes(adapters_ref[...], table_ref[...], per_owner)
    owner = jnp.concatenate([column_of(owner)] * steps, axis=0)
    place = jnp.concatenate([column_of(place)] * steps, axis=0)
    shape = spread_ref.shape
    slot = iota(shape, 1)
    slot_owner = slot // rows
    slot_step = (slot - slot_owner * rows) // capacity
    slot_place = slot - slot_owner * rows - slot_step * capacity
    hit = (
        (slot_owner == owner)
        & (slot_place == place)
        & (slot_step == iota(shape, 0) // requests)
    )
    spread_ref[...] = jnp.where(hit, 1.0, 0.0).astype(BF)

    length = column_of(lengths_ref[...])
    position = jnp.concatenate([length + step for step in range(steps)], axis=0)
    angle = position.astype(F32) * freq_ref[...]
    cosine = jnp.cos(angle)
    sine = jnp.sin(angle)
    half = angle.shape[1] // 2
    sine = jnp.where(iota(angle.shape, 1) < half, -sine, sine)
    cosine_ref[...] = cosine
    sine_ref[...] = sine

    out_ref[...] = jnp.zeros_like(out_ref)

    @pl.loop(0, parts)
    def _(part):
        part_copy(part).wait()
        span = pl.ds(pl.multiple_of(part * depth, depth), depth)
        out_ref[...] += jnp.dot(
            states_ref[:, span], weight[span, :], preferred_element_type=F32
        )

    new_copy.wait()
    fresh = jnp.dot(states_ref[...], new_weight[...], preferred_element_type=F32)
    turned = fresh * cosine_ref[...] + pltpu.roll(fresh, half, 1) * sine_ref[...]
    is_first = lax.axis_index("tensor") % 2 == 0
    piece_ref[...] = jnp.where(is_first, turned, fresh).astype(BF)


def load_kernel(source, after, out_ref, sem):
    copy = pltpu.make_async_copy(source, out_ref, sem.at[0])
    copy.start()
    copy.wait()


def query_kernel(
    dims, terms_ref, spread_ref, projected_ref, piece_ref, cosine_ref, sine_ref, first_ref, second_ref, packed
):
    steps, requests, heads, head_width = dims
    correction = jnp.dot(spread_ref[...], terms_ref[...], preferred_element_type=F32)
    query = projected_ref[...] + ADAPTER_SCALE * correction
    cosine = cosine_ref[...]
    sine = sine_ref[...]
    count = packed.shape[0]
    for head in range(heads):
        vector = query[:, head * head_width : (head + 1) * head_width]
        vector = vector * cosine + pltpu.roll(vector, head_width // 2, 1) * sine
        for step in range(steps):
            packed[pl.ds(step * heads + head, requests, stride=steps * heads), :] = vector[
                step * requests : (step + 1) * requests
            ]
    half = count // 2
    first_ref[:half, :] = packed[:half, :].astype(BF)
    first_ref[half:, :] = piece_ref[...]
    second_ref[...] = packed[half:, :].astype(BF)


def attend(dims, first_request, lengths_ref, query_ref, cache_ref, keys, vals, scratch, store):
    steps, requests, heads, head_width, kv_split = dims
    scores_ref, recent_ref, weights_ref, new_weights_ref, acc_ref = scratch
    per_request = steps * heads
    mine = requests // 2
    count = mine * per_request
    scale = head_width ** (-0.5)
    context = cache_ref.shape[2]
    part = lax.axis_index("tensor") % kv_split
    base = part * context
    lane = iota((per_request, context), 1)
    for request in range(mine):
        span = pl.ds(request * per_request, per_request)
        score = lax.dot_general(
            query_ref[span, :],
            cache_ref[first_request + request, 0],
            (((1,), (1,)), ((), ())),
            preferred_element_type=F32,
        )
        scores_ref[span, :] = jnp.where(
            lane < lengths_ref[first_request + request] - base, score * scale, MASKED
        )
    rows = min(128, count)
    shape = (rows, steps * requests)
    column_step = iota(shape, 1) // requests
    column_request = iota(shape, 1) - column_step * requests
    row_request = iota(shape, 0) // per_request
    row_step = (iota(shape, 0) - row_request * per_request) // heads
    allowed = (column_step <= row_step) & (part == 0)
    ahead = column_request - row_request
    for at in range(count // rows):
        span = pl.ds(at * rows, rows)
        recent = lax.dot_general(
            query_ref[span, :], keys, (((1,), (1,)), ((), ())), preferred_element_type=F32
        )
        recent_ref[span, :] = jnp.where(
            allowed & (ahead == first_request + at * (rows // per_request)), recent * scale, MASKED
        )
    totals = []
    for at in range(count // rows):
        span = pl.ds(at * rows, rows)
        scores = scores_ref[span, :]
        recent = recent_ref[span, :]
        top = jnp.maximum(
            jnp.max(scores, axis=1, keepdims=True), jnp.max(recent, axis=1, keepdims=True)
        ) if scores.shape != recent.shape else jnp.max(
            jnp.maximum(scores, recent), axis=1, keepdims=True
        )
        e_cached = jnp.exp(scores - top)
        e_recent = jnp.exp(recent - top)
        total = (
            jnp.sum(e_cached, axis=1, keepdims=True) + jnp.sum(e_recent, axis=1, keepdims=True)
            if scores.shape != recent.shape
            else jnp.sum(e_cached + e_recent, axis=1, keepdims=True)
        )
        weights_ref[span, :] = e_cached.astype(BF)
        new_weights_ref[span, :] = e_recent.astype(BF)
        totals.append((top, total))
    for request in range(mine):
        span = pl.ds(request * per_request, per_request)
        acc_ref[span, :] = jnp.dot(
            weights_ref[span, :],
            cache_ref[first_request + request, 1],
            preferred_element_type=F32,
        )
    for at in range(count // rows):
        span = pl.ds(at * rows, rows)
        top, total = totals[at]
        acc = acc_ref[span, :] + jnp.dot(
            new_weights_ref[span, :], vals, preferred_element_type=F32
        )
        store(at, rows, acc * (1.0 / total), top + jnp.log(total))


def new_pieces(own, other):
    first = lax.axis_index("tensor") % 2 == 0
    keys = jnp.where(first, own.astype(F32), other.astype(F32)).astype(BF)
    vals = jnp.where(first, other.astype(F32), own.astype(F32)).astype(BF)
    return keys, vals


def own_kernel(
    dims, first, lengths_ref, sent_ref, got_ref, query_ref, cache_ref, out_ref, level_ref, *scratch
):
    count = out_ref.shape[0]
    keys, vals = new_pieces(sent_ref[count:, :], got_ref[count:, :])

    def store(at, rows, result, level):
        out_ref[pl.ds(at * rows, rows), :] = result
        level_ref[pl.ds(at * rows, rows), :] = level

    attend(dims, first, lengths_ref, query_ref, cache_ref, keys, vals, scratch, store)


def send_kernel(
    dims, first, lengths_ref, sent_ref, got_ref, query_ref, cache_ref, out_ref, levels, *scratch
):
    lines = levels.shape[0]
    count = lines * 128
    keys, vals = new_pieces(sent_ref[count:, :], got_ref[count:, :])

    def store(at, rows, result, level):
        out_ref[pl.ds(at * rows, rows), :] = result.astype(BF)
        for line in range(rows // 128):
            levels[pl.ds(at * (rows // 128) + line, 1), :] = row_of(
                level[line * 128 : (line + 1) * 128]
            )

    attend(dims, first, lengths_ref, query_ref, cache_ref, keys, vals, scratch, store)
    rest = levels[...]
    pieces = []
    for _ in range(3):
        piece = rest.astype(BF)
        pieces.append(piece)
        rest = rest - piece.astype(F32)
    pieces.append(jnp.zeros_like(pieces[0]))
    out_ref[pl.ds(count, 4 * lines), :] = jnp.concatenate(pieces, axis=0)


def merge_kernel(dims, *refs):
    steps, requests, heads, head_width = dims
    out_ref, packed = refs[6:]
    for half in range(2):
        own_ref, level_ref, got_ref = refs[3 * half : 3 * half + 3]
        count = own_ref.shape[0]
        lines = count // 128
        extra = got_ref[pl.ds(count, 4 * lines), :].astype(F32)
        other_level = extra[:lines] + extra[lines : 2 * lines] + extra[2 * lines : 3 * lines]
        for line in range(lines):
            span = pl.ds(line * 128, 128)
            theirs = column_of(other_level[line : line + 1])
            mine = level_ref[span, :]
            top = jnp.maximum(mine, theirs)
            mine = jnp.exp(mine - top)
            theirs = jnp.exp(theirs - top)
            total = mine + theirs
            packed[pl.ds(half * count + line * 128, 128), :] = own_ref[span, :] * (
                mine / total
            ) + got_ref[span, :].astype(F32) * (theirs / total)
    for step in range(steps):
        for head in range(heads):
            out_ref[
                step * requests : (step + 1) * requests,
                head * head_width : (head + 1) * head_width,
            ] = packed[pl.ds(step * heads + head, requests, stride=steps * heads), :].astype(BF)


def in_vmem(shape, dtype):
    return pltpu.VMEM(shape, dtype)


def in_hbm(value):
    return pltpu.with_memory_space_constraint(value, pltpu.HBM)


def vmem_limit(mebibytes):
    return pltpu.CompilerParams(vmem_limit_bytes=mebibytes * 2**20)


def whole(*refs):
    return [pl.BlockSpec(memory_space=pltpu.VMEM)] * len(refs)


def local(
    inputs,
    query_weight,
    key_value_weight,
    key_value_cache,
    lengths,
    request_adapter,
    adapter_storage_row,
    adapter_down_factors,
    adapter_up_factors,
):
    steps, requests, width = inputs.shape
    tensor_count = lax.axis_size("tensor")
    pool_count = lax.axis_size("pool")
    owners = tensor_count * pool_count
    head_width = key_value_cache.shape[-1]
    context = key_value_cache.shape[-2]
    kv_split = 2 * head_width // key_value_weight.shape[1]
    query_columns = query_weight.shape[1]
    heads = query_columns // head_width
    per_owner, rank, _ = adapter_down_factors.shape
    capacity = max(2, 2 * requests // owners)
    rows = steps * capacity
    count = steps * requests

    flat = inputs.reshape(count, width)
    adapters = request_adapter.reshape(1, requests)
    table = adapter_storage_row.reshape(1, -1)
    down = adapter_down_factors.reshape(per_owner * rank, width)
    up = adapter_up_factors.reshape(per_owner * rank, -1)
    cache = key_value_cache.reshape(requests, 2, context, head_width)
    anywhere = pl.BlockSpec(memory_space=pltpu.HBM)
    smem = pl.BlockSpec(memory_space=pltpu.SMEM)

    quarter = per_owner * rank // 4
    lora_dims = (steps, requests, capacity, per_owner, pool_count)
    flat_here, down_first, adapters, table, own, own_rows, others, others_rows = pl.pallas_call(
        functools.partial(stage_kernel, lora_dims),
        out_shape=[
            in_vmem(flat.shape, BF),
            in_vmem((quarter, width), BF),
            in_vmem(adapters.shape, I32),
            in_vmem(table.shape, I32),
            in_vmem((rows, width), BF),
            in_vmem((rows, 1), I32),
            in_vmem((rows, width), BF),
            in_vmem((rows, 1), I32),
        ],
        in_specs=[anywhere] * 4,
        out_specs=whole(*range(8)),
        scratch_shapes=[pltpu.SemaphoreType.DMA((2,)), pltpu.SemaphoreType.DMA((3,))],
        compiler_params=vmem_limit(8),
        name="stage",
    )(in_hbm(flat), in_hbm(down), in_hbm(adapters), in_hbm(table))
    others = swapped(others, "pool", 0)
    others_rows = swapped(others_rows, "pool", 0)

    down_second = pl.pallas_call(
        functools.partial(more_kernel, quarter),
        out_shape=in_vmem((2 * quarter, width), BF),
        in_specs=[anywhere, pl.BlockSpec(memory_space=pl.ANY)],
        out_specs=whole(0)[0],
        scratch_shapes=[pltpu.SemaphoreType.DMA((4,))],
        compiler_params=vmem_limit(1),
        cost_estimate=pl.CostEstimate(flops=0, bytes_accessed=2 * down.size, transcendentals=0),
        name="more",
    )(in_hbm(down), own_rows)

    outgoing = pl.pallas_call(
        functools.partial(lora_kernel, lora_dims, rank),
        out_shape=jax.ShapeDtypeStruct((owners, rows, query_columns), BF),
        in_specs=whole(*range(6)) + [anywhere] * 2,
        out_specs=whole(0)[0],
        scratch_shapes=[
            pltpu.VMEM((quarter, width), BF),
            pltpu.VMEM(up.shape, BF),
            pltpu.VMEM((2 * rows, per_owner * rank), BF),
            pltpu.SemaphoreType.DMA((1,)),
            pltpu.SemaphoreType.DMA((tensor_count,)),
        ],
        compiler_params=vmem_limit(28),
        cost_estimate=pl.CostEstimate(
            flops=8 * rows * per_owner * rank * width,
            bytes_accessed=2 * per_owner * rank * width,
            transcendentals=0,
        ),
        name="lora",
    )(
        own,
        own_rows,
        pltpu.with_memory_space_constraint(others, pltpu.VMEM),
        pltpu.with_memory_space_constraint(others_rows, pltpu.VMEM),
        down_first,
        down_second,
        in_hbm(down),
        in_hbm(up),
    )
    terms = lax.all_to_all(outgoing, ("tensor", "pool"), split_axis=0, concat_axis=0, tiled=True)
    terms = terms.reshape(owners * rows, query_columns)

    flat_late, adapters, table, _ = lax.optimization_barrier(
        (flat_here, adapters, table, outgoing)
    )
    power = np.arange(head_width // 2, dtype=np.float64) * (-2.0 / head_width)
    freq = np.tile(ROPE_BASE**power, 2).astype(np.float32).reshape(1, head_width)
    projected, own_piece, cosine, sine, spread = pl.pallas_call(
        functools.partial(project_kernel, (steps, requests, capacity, per_owner)),
        out_shape=[
            in_vmem((count, query_columns), F32),
            in_vmem((count, head_width), BF),
            in_vmem((count, head_width), F32),
            in_vmem((count, head_width), F32),
            in_vmem((count, owners * rows), BF),
        ],
        in_specs=whole(*range(5)) + [anywhere] * 2,
        out_specs=whole(*range(5)),
        scratch_shapes=[
            pltpu.VMEM(query_weight.shape, BF),
            pltpu.VMEM(key_value_weight.shape, BF),
            pltpu.SemaphoreType.DMA((17,)),
        ],
        compiler_params=vmem_limit(28),
        cost_estimate=pl.CostEstimate(
            flops=2 * count * width * query_columns,
            bytes_accessed=2 * width * query_columns,
            transcendentals=0,
        ),
        name="project",
    )(
        flat_late,
        adapters,
        table,
        lengths.reshape(1, requests),
        jnp.asarray(freq),
        in_hbm(query_weight),
        in_hbm(key_value_weight),
    )

    dims = (steps, requests, heads, head_width)
    packed_rows = count * heads
    half_rows = packed_rows // 2
    sent, sent_second = pl.pallas_call(
        functools.partial(query_kernel, dims),
        out_shape=[
            jax.ShapeDtypeStruct((half_rows + count, head_width), BF),
            jax.ShapeDtypeStruct((half_rows, head_width), BF),
        ],
        in_specs=whole(*range(6)),
        out_specs=whole(*range(2)),
        scratch_shapes=[pltpu.VMEM((packed_rows, head_width), F32)],
        compiler_params=vmem_limit(8),
        name="query",
    )(terms, spread, projected, own_piece, cosine, sine)
    got = swapped(sent, "tensor", 0)
    got_second = swapped(sent_second, "tensor", 0)

    cache_here = pl.pallas_call(
        load_kernel,
        out_shape=in_vmem(cache.shape, BF),
        in_specs=[anywhere, pl.BlockSpec(memory_space=pl.ANY)],
        out_specs=whole(0)[0],
        scratch_shapes=[pltpu.SemaphoreType.DMA((1,))],
        compiler_params=vmem_limit(1),
        cost_estimate=pl.CostEstimate(
            flops=0, bytes_accessed=4 * cache.size, transcendentals=0
        ),
        name="load",
    )(in_hbm(cache), sent)

    lines = half_rows // 128
    attend_dims = (steps, requests, heads, head_width, kv_split)
    attend_scratch = [
        pltpu.VMEM((half_rows, context), F32),
        pltpu.VMEM((half_rows, count), F32),
        pltpu.VMEM((half_rows, context), BF),
        pltpu.VMEM((half_rows, count), BF),
        pltpu.VMEM((half_rows, head_width), F32),
    ]
    cost = pl.CostEstimate(
        flops=2 * packed_rows * context * head_width,
        bytes_accessed=cache.size,
        transcendentals=half_rows * context,
    )
    partials = []
    sending = None
    for half, other_query in enumerate((got, got_second)):
        sending = pl.pallas_call(
            functools.partial(send_kernel, attend_dims, half * (requests // 2)),
            out_shape=jax.ShapeDtypeStruct((half_rows + 4 * lines, head_width), BF),
            in_specs=[smem] + whole(*range(4)),
            out_specs=whole(0)[0],
            scratch_shapes=[pltpu.VMEM((lines, 128), F32)] + attend_scratch,
            compiler_params=vmem_limit(16),
            cost_estimate=cost,
            name="send",
        )(lengths, sent, got, other_query, cache_here)
        partials.append(swapped(sending, "tensor", 0))
    queries = lax.optimization_barrier((sent, sent_second, sending))
    merging = []
    for half in range(2):
        own, level = pl.pallas_call(
            functools.partial(own_kernel, attend_dims, half * (requests // 2)),
            out_shape=[
                jax.ShapeDtypeStruct((half_rows, head_width), F32),
                jax.ShapeDtypeStruct((half_rows, 1), F32),
            ],
            in_specs=[smem] + whole(*range(4)),
            out_specs=whole(*range(2)),
            scratch_shapes=attend_scratch,
            compiler_params=vmem_limit(16),
            cost_estimate=cost,
            name="own",
        )(lengths, sent, got, queries[half], cache_here)
        merging += [own, level, partials[half]]
    attended = pl.pallas_call(
        functools.partial(merge_kernel, dims),
        out_shape=jax.ShapeDtypeStruct((count, query_columns), BF),
        in_specs=whole(*range(6)),
        out_specs=whole(0)[0],
        scratch_shapes=[pltpu.VMEM((packed_rows, head_width), F32)],
        compiler_params=vmem_limit(8),
        name="merge",
    )(*merging)
    return attended.reshape(steps, requests, query_columns)


def solution(mesh):
    placed = (
        P(None, ("groups", "pool"), None),
        P(None, "tensor"),
        P(None, "tensor"),
        P(("groups", "pool"), "tensor", None, None, None),
        P(("groups", "pool")),
        P(("groups", "pool")),
        P("groups"),
        P(("groups", "tensor", "pool"), None, None),
        P(("groups", "tensor", "pool"), None, None),
    )
    return jax.shard_map(
        local,
        mesh=mesh,
        in_specs=placed,
        out_specs=P(None, ("groups", "pool"), "tensor"),
        check_vma=False,
    )
```

```python
import functools

import jax
import jax.numpy as jnp
import numpy as np
from jax import lax
from jax.experimental import pallas as pl
from jax.experimental.pallas import tpu as pltpu
from jax.sharding import PartitionSpec as P

ROPE_BASE = 500000.0
ADAPTER_SCALE = 0.5
MASKED = -1e30
BF = jnp.bfloat16
F32 = jnp.float32
I32 = jnp.int32


def swapped(value, axis, bit):
    mask = 2**bit
    pairs = [(source, source ^ mask) for source in range(lax.axis_size(axis))]
    return lax.ppermute(value, axis, pairs)


def iota(shape, axis):
    return lax.broadcasted_iota(I32, shape, axis)


def column_of(row):
    count = row.shape[1]
    eye = iota((count, count), 0) == iota((count, count), 1)
    return jnp.sum(jnp.where(eye, row, jnp.zeros_like(row)), axis=1, keepdims=True)


def row_of(column):
    count = column.shape[0]
    eye = iota((count, count), 0) == iota((count, count), 1)
    return jnp.sum(jnp.where(eye, column, jnp.zeros_like(column)), axis=0, keepdims=True)


def routes(adapters, table, per_owner):
    requests = adapters.shape[1]
    rows = table.shape[1]
    match = (iota((rows, requests), 0) == adapters).astype(F32)
    stored = jnp.dot(
        table.astype(F32), match, precision=lax.Precision.HIGHEST, preferred_element_type=F32
    ).astype(I32)
    owner = stored // per_owner
    local_row = stored - owner * per_owner
    owner_column = column_of(owner)
    ahead = iota((requests, requests), 0) < iota((requests, requests), 1)
    place = jnp.sum(
        jnp.where((owner_column == owner) & ahead, 1, 0), axis=0, keepdims=True
    )
    return owner, local_row, place


def picked(dims, pools, states_ref, adapters, table):
    steps, requests, capacity, per_owner, pool_count = dims
    owner, local_row, place = routes(adapters, table, per_owner)
    owner = jnp.concatenate([owner] * steps, axis=1)
    place = jnp.concatenate([place] * steps, axis=1)
    local_row = jnp.concatenate([local_row] * steps, axis=1)
    shape = (steps * capacity, steps * requests)
    row = iota(shape, 0)
    row_step = row // capacity
    slot = (place == row - row_step * capacity) & (row_step == iota(shape, 1) // requests)
    hits = [
        slot & (owner == lax.axis_index("tensor") * pool_count + pool) for pool in pools
    ]
    pick = jnp.concatenate([jnp.where(hit, 1.0, 0.0) for hit in hits], axis=0).astype(BF)
    states = jnp.dot(pick, states_ref[...], preferred_element_type=F32).astype(BF)
    rows = [jnp.sum(jnp.where(hit, local_row, 0), axis=1, keepdims=True) for hit in hits]
    return states, rows


def stage_kernel(dims, states_hbm, down_hbm, adapters_hbm, table_hbm, *rest):
    states, down, adapters, table, own, own_rows, other, other_rows, sem, other_sem = rest
    parts = sem.shape[0]
    size = down.shape[0] // parts
    first = [
        pltpu.make_async_copy(adapters_hbm, adapters, other_sem.at[1]),
        pltpu.make_async_copy(table_hbm, table, other_sem.at[2]),
        pltpu.make_async_copy(states_hbm, states, other_sem.at[0]),
    ]
    copies = []
    for part in range(parts):
        span = pl.ds(part * size, size)
        copies.append(pltpu.make_async_copy(down_hbm.at[span], down.at[span], sem.at[part]))
    for copy in first + copies:
        copy.start()
    for copy in first:
        copy.wait()
    pool = lax.axis_index("pool")
    chosen, rows = picked(dims, (pool, 1 - pool), states, adapters[...], table[...])
    count = own.shape[0]
    own[...] = chosen[:count]
    other[...] = chosen[count:]
    own_rows[...] = rows[0]
    other_rows[...] = rows[1]
    for copy in copies:
        copy.wait()


def more_kernel(first_row, down_hbm, after, down, sem):
    parts = sem.shape[0]
    size = down.shape[0] // parts
    copies = [
        pltpu.make_async_copy(
            down_hbm.at[pl.ds(first_row + part * size, size)],
            down.at[pl.ds(part * size, size)],
            sem.at[part],
        )
        for part in range(parts)
    ]
    for copy in copies:
        copy.start()
    for copy in copies:
        copy.wait()


def lora_kernel(
    dims,
    rank,
    own_ref,
    own_rows_ref,
    other_ref,
    other_rows_ref,
    down_first,
    down_second,
    down_hbm,
    up_hbm,
    out_ref,
    down_rest,
    up,
    low,
    down_sem,
    up_sem,
):
    steps, requests, capacity, per_owner, pool_count = dims
    rows = steps * capacity
    here_rows = down_first.shape[0] + down_second.shape[0]
    down_rows = down_rest.shape[0]
    up_parts = up_sem.shape[0]
    up_columns = up.shape[1] // up_parts
    rest_copy = pltpu.make_async_copy(
        down_hbm.at[pl.ds(here_rows, down_rows)], down_rest, down_sem.at[0]
    )

    def up_copy(part):
        columns = pl.ds(pl.multiple_of(part * up_columns, up_columns), up_columns)
        return pltpu.make_async_copy(
            up_hbm.at[:, columns], up.at[:, columns], up_sem.at[part]
        )

    rest_copy.start()

    @pl.loop(0, up_parts)
    def _(part):
        up_copy(part).start()

    pool = lax.axis_index("pool")
    local_rows = jnp.concatenate([own_rows_ref[...], other_rows_ref[...]], axis=0)
    states = jnp.concatenate([own_ref[...].astype(F32), other_ref[...].astype(F32)], axis=0).T.astype(BF)

    def factors_of(rows_ref, first_row):
        count = rows_ref.shape[0]
        piece = lax.dot_general(
            rows_ref[...], states, (((1,), (0,)), ((), ())), preferred_element_type=F32
        ).T
        holder = (iota(piece.shape, 1) + first_row) // rank
        low[:, pl.ds(first_row, count)] = jnp.where(
            holder == local_rows, piece.astype(BF), jnp.zeros(piece.shape, BF)
        )

    first_row = 0
    for staged in (down_first, down_second):
        for at in range(0, staged.shape[0], down_rows):
            factors_of(staged.at[pl.ds(at, down_rows)], first_row)
            first_row += down_rows

    @pl.loop(0, 1)
    def _(_):
        rest_copy.wait()

    factors_of(down_rest, here_rows)
    factors = low[...]
    for part in range(up_parts):
        up_copy(part).wait()
        columns = pl.ds(part * up_columns, up_columns)
        term = jnp.dot(factors, up[:, columns], preferred_element_type=F32).astype(BF)
        out_ref[part * pool_count + pool] = term[:rows]
        out_ref[part * pool_count + 1 - pool] = term[rows:]


def project_kernel(
    dims,
    states_ref,
    adapters_ref,
    table_ref,
    lengths_ref,
    freq_ref,
    weight_hbm,
    new_weight_hbm,
    out_ref,
    piece_ref,
    cosine_ref,
    sine_ref,
    spread_ref,
    weight,
    new_weight,
    sem,
):
    steps, requests, capacity, per_owner = dims
    parts = sem.shape[0] - 1
    depth = weight.shape[0] // parts
    new_copy = pltpu.make_async_copy(new_weight_hbm, new_weight, sem.at[parts])

    def part_copy(part):
        span = pl.ds(pl.multiple_of(part * depth, depth), depth)
        return pltpu.make_async_copy(weight_hbm.at[span], weight.at[span], sem.at[part])

    @pl.loop(0, parts)
    def _(part):
        part_copy(part).start()

    new_copy.start()

    rows = steps * capacity
    owner, _, place = routes(adapters_ref[...], table_ref[...], per_owner)
    owner = jnp.concatenate([column_of(owner)] * steps, axis=0)
    place = jnp.concatenate([column_of(place)] * steps, axis=0)
    shape = spread_ref.shape
    slot = iota(shape, 1)
    slot_owner = slot // rows
    slot_step = (slot - slot_owner * rows) // capacity
    slot_place = slot - slot_owner * rows - slot_step * capacity
    hit = (
        (slot_owner == owner)
        & (slot_place == place)
        & (slot_step == iota(shape, 0) // requests)
    )
    spread_ref[...] = jnp.where(hit, 1.0, 0.0).astype(BF)

    length = column_of(lengths_ref[...])
    position = jnp.concatenate([length + step for step in range(steps)], axis=0)
    angle = position.astype(F32) * freq_ref[...]
    cosine = jnp.cos(angle)
    sine = jnp.sin(angle)
    half = angle.shape[1] // 2
    sine = jnp.where(iota(angle.shape, 1) < half, -sine, sine)
    cosine_ref[...] = cosine
    sine_ref[...] = sine

    out_ref[...] = jnp.zeros_like(out_ref)

    @pl.loop(0, parts)
    def _(part):
        part_copy(part).wait()
        span = pl.ds(pl.multiple_of(part * depth, depth), depth)
        out_ref[...] += jnp.dot(
            states_ref[:, span], weight[span, :], preferred_element_type=F32
        )

    new_copy.wait()
    fresh = jnp.dot(states_ref[...], new_weight[...], preferred_element_type=F32)
    turned = fresh * cosine_ref[...] + pltpu.roll(fresh, half, 1) * sine_ref[...]
    is_first = lax.axis_index("tensor") % 2 == 0
    piece_ref[...] = jnp.where(is_first, turned, fresh).astype(BF)


def load_kernel(source, after, out_ref, sem):
    copy = pltpu.make_async_copy(source, out_ref, sem.at[0])
    copy.start()
    copy.wait()


def query_kernel(
    dims, terms_ref, spread_ref, projected_ref, piece_ref, cosine_ref, sine_ref, first_ref, second_ref, packed
):
    steps, requests, heads, head_width = dims
    correction = jnp.dot(spread_ref[...], terms_ref[...], preferred_element_type=F32)
    query = projected_ref[...] + ADAPTER_SCALE * correction
    cosine = cosine_ref[...]
    sine = sine_ref[...]
    count = packed.shape[0]
    for head in range(heads):
        vector = query[:, head * head_width : (head + 1) * head_width]
        vector = vector * cosine + pltpu.roll(vector, head_width // 2, 1) * sine
        for step in range(steps):
            packed[pl.ds(step * heads + head, requests, stride=steps * heads), :] = vector[
                step * requests : (step + 1) * requests
            ]
    half = count // 2
    first_ref[:half, :] = packed[:half, :].astype(BF)
    first_ref[half:, :] = piece_ref[...]
    second_ref[...] = packed[half:, :].astype(BF)


def attend(dims, first_request, lengths_ref, query_ref, cache_ref, keys, vals, scratch, store):
    steps, requests, heads, head_width, kv_split = dims
    scores_ref, recent_ref, weights_ref, new_weights_ref, acc_ref = scratch
    per_request = steps * heads
    mine = requests // 2
    count = mine * per_request
    scale = head_width ** (-0.5)
    context = cache_ref.shape[2]
    part = lax.axis_index("tensor") % kv_split
    base = part * context
    lane = iota((per_request, context), 1)
    for request in range(mine):
        span = pl.ds(request * per_request, per_request)
        score = lax.dot_general(
            query_ref[span, :],
            cache_ref[first_request + request, 0],
            (((1,), (1,)), ((), ())),
            preferred_element_type=F32,
        )
        scores_ref[span, :] = jnp.where(
            lane < lengths_ref[first_request + request] - base, score * scale, MASKED
        )
    rows = min(128, count)
    shape = (rows, steps * requests)
    column_step = iota(shape, 1) // requests
    column_request = iota(shape, 1) - column_step * requests
    row_request = iota(shape, 0) // per_request
    row_step = (iota(shape, 0) - row_request * per_request) // heads
    allowed = (column_step <= row_step) & (part == 0)
    ahead = column_request - row_request
    for at in range(count // rows):
        span = pl.ds(at * rows, rows)
        recent = lax.dot_general(
            query_ref[span, :], keys, (((1,), (1,)), ((), ())), preferred_element_type=F32
        )
        recent_ref[span, :] = jnp.where(
            allowed & (ahead == first_request + at * (rows // per_request)), recent * scale, MASKED
        )
    totals = []
    for at in range(count // rows):
        span = pl.ds(at * rows, rows)
        scores = scores_ref[span, :]
        recent = recent_ref[span, :]
        top = jnp.maximum(
            jnp.max(scores, axis=1, keepdims=True), jnp.max(recent, axis=1, keepdims=True)
        ) if scores.shape != recent.shape else jnp.max(
            jnp.maximum(scores, recent), axis=1, keepdims=True
        )
        e_cached = jnp.exp(scores - top)
        e_recent = jnp.exp(recent - top)
        total = (
            jnp.sum(e_cached, axis=1, keepdims=True) + jnp.sum(e_recent, axis=1, keepdims=True)
            if scores.shape != recent.shape
            else jnp.sum(e_cached + e_recent, axis=1, keepdims=True)
        )
        weights_ref[span, :] = e_cached.astype(BF)
        new_weights_ref[span, :] = e_recent.astype(BF)
        totals.append((top, total))
    for request in range(mine):
        span = pl.ds(request * per_request, per_request)
        acc_ref[span, :] = jnp.dot(
            weights_ref[span, :],
            cache_ref[first_request + request, 1],
            preferred_element_type=F32,
        )
    for at in range(count // rows):
        span = pl.ds(at * rows, rows)
        top, total = totals[at]
        acc = acc_ref[span, :] + jnp.dot(
            new_weights_ref[span, :], vals, preferred_element_type=F32
        )
        store(at, rows, acc * (1.0 / total), top + jnp.log(total))


def new_pieces(own, other):
    first = lax.axis_index("tensor") % 2 == 0
    keys = jnp.where(first, own.astype(F32), other.astype(F32)).astype(BF)
    vals = jnp.where(first, other.astype(F32), own.astype(F32)).astype(BF)
    return keys, vals


def own_kernel(
    dims, first, lengths_ref, sent_ref, got_ref, query_ref, cache_ref, out_ref, level_ref, *scratch
):
    count = out_ref.shape[0]
    keys, vals = new_pieces(sent_ref[count:, :], got_ref[count:, :])

    def store(at, rows, result, level):
        out_ref[pl.ds(at * rows, rows), :] = result
        for line in range(rows // 128):
            level_ref[pl.ds(at * (rows // 128) + line, 1), :] = row_of(
                level[line * 128 : (line + 1) * 128]
            )

    attend(dims, first, lengths_ref, query_ref, cache_ref, keys, vals, scratch, store)


def send_kernel(
    dims, first, lengths_ref, sent_ref, got_ref, query_ref, cache_ref, out_ref, levels, *scratch
):
    lines = levels.shape[0]
    count = lines * 128
    keys, vals = new_pieces(sent_ref[count:, :], got_ref[count:, :])

    def store(at, rows, result, level):
        out_ref[pl.ds(at * rows, rows), :] = result.astype(BF)
        for line in range(rows // 128):
            levels[pl.ds(at * (rows // 128) + line, 1), :] = row_of(
                level[line * 128 : (line + 1) * 128]
            )

    attend(dims, first, lengths_ref, query_ref, cache_ref, keys, vals, scratch, store)
    rest = levels[...]
    pieces = []
    for _ in range(3):
        piece = rest.astype(BF)
        pieces.append(piece)
        rest = rest - piece.astype(F32)
    pieces.append(jnp.zeros_like(pieces[0]))
    out_ref[pl.ds(count, 4 * lines), :] = jnp.concatenate(pieces, axis=0)


def merge_kernel(dims, *refs):
    steps, requests, heads, head_width = dims
    out_ref, packed = refs[6:]
    for half in range(2):
        own_ref, level_ref, got_ref = refs[3 * half : 3 * half + 3]
        count = own_ref.shape[0]
        lines = count // 128
        extra = got_ref[pl.ds(count, 4 * lines), :].astype(F32)
        theirs = extra[:lines] + extra[lines : 2 * lines] + extra[2 * lines : 3 * lines]
        mine = level_ref[...]
        top = jnp.maximum(mine, theirs)
        mine = jnp.exp(mine - top)
        theirs = jnp.exp(theirs - top)
        total = mine + theirs
        mine = mine / total
        theirs = theirs / total
        for line in range(lines):
            span = pl.ds(line * 128, 128)
            packed[pl.ds(half * count + line * 128, 128), :] = own_ref[span, :] * column_of(
                mine[line : line + 1]
            ) + got_ref[span, :].astype(F32) * column_of(theirs[line : line + 1])
    for step in range(steps):
        for head in range(heads):
            out_ref[
                step * requests : (step + 1) * requests,
                head * head_width : (head + 1) * head_width,
            ] = packed[pl.ds(step * heads + head, requests, stride=steps * heads), :].astype(BF)


def in_vmem(shape, dtype):
    return pltpu.VMEM(shape, dtype)


def in_hbm(value):
    return pltpu.with_memory_space_constraint(value, pltpu.HBM)


def vmem_limit(mebibytes):
    return pltpu.CompilerParams(vmem_limit_bytes=mebibytes * 2**20)


def whole(*refs):
    return [pl.BlockSpec(memory_space=pltpu.VMEM)] * len(refs)


def local(
    inputs,
    query_weight,
    key_value_weight,
    key_value_cache,
    lengths,
    request_adapter,
    adapter_storage_row,
    adapter_down_factors,
    adapter_up_factors,
):
    steps, requests, width = inputs.shape
    tensor_count = lax.axis_size("tensor")
    pool_count = lax.axis_size("pool")
    owners = tensor_count * pool_count
    head_width = key_value_cache.shape[-1]
    context = key_value_cache.shape[-2]
    kv_split = 2 * head_width // key_value_weight.shape[1]
    query_columns = query_weight.shape[1]
    heads = query_columns // head_width
    per_owner, rank, _ = adapter_down_factors.shape
    capacity = max(2, 2 * requests // owners)
    rows = steps * capacity
    count = steps * requests

    flat = inputs.reshape(count, width)
    adapters = request_adapter.reshape(1, requests)
    table = adapter_storage_row.reshape(1, -1)
    down = adapter_down_factors.reshape(per_owner * rank, width)
    up = adapter_up_factors.reshape(per_owner * rank, -1)
    cache = key_value_cache.reshape(requests, 2, context, head_width)
    anywhere = pl.BlockSpec(memory_space=pltpu.HBM)
    smem = pl.BlockSpec(memory_space=pltpu.SMEM)

    quarter = per_owner * rank // 4
    lora_dims = (steps, requests, capacity, per_owner, pool_count)
    flat_here, down_first, adapters, table, own, own_rows, others, others_rows = pl.pallas_call(
        functools.partial(stage_kernel, lora_dims),
        out_shape=[
            in_vmem(flat.shape, BF),
            in_vmem((2 * quarter, width), BF),
            in_vmem(adapters.shape, I32),
            in_vmem(table.shape, I32),
            in_vmem((rows, width), BF),
            in_vmem((rows, 1), I32),
            in_vmem((rows, width), BF),
            in_vmem((rows, 1), I32),
        ],
        in_specs=[anywhere] * 4,
        out_specs=whole(*range(8)),
        scratch_shapes=[pltpu.SemaphoreType.DMA((2,)), pltpu.SemaphoreType.DMA((3,))],
        compiler_params=vmem_limit(8),
        name="stage",
    )(in_hbm(flat), in_hbm(down), in_hbm(adapters), in_hbm(table))
    others = swapped(others, "pool", 0)
    others_rows = swapped(others_rows, "pool", 0)

    down_second = pl.pallas_call(
        functools.partial(more_kernel, 2 * quarter),
        out_shape=in_vmem((quarter, width), BF),
        in_specs=[anywhere, pl.BlockSpec(memory_space=pl.ANY)],
        out_specs=whole(0)[0],
        scratch_shapes=[pltpu.SemaphoreType.DMA((4,))],
        compiler_params=vmem_limit(1),
        cost_estimate=pl.CostEstimate(flops=0, bytes_accessed=2 * down.size, transcendentals=0),
        name="more",
    )(in_hbm(down), own_rows)

    outgoing = pl.pallas_call(
        functools.partial(lora_kernel, lora_dims, rank),
        out_shape=jax.ShapeDtypeStruct((owners, rows, query_columns), BF),
        in_specs=whole(*range(6)) + [anywhere] * 2,
        out_specs=whole(0)[0],
        scratch_shapes=[
            pltpu.VMEM((quarter, width), BF),
            pltpu.VMEM(up.shape, BF),
            pltpu.VMEM((2 * rows, per_owner * rank), BF),
            pltpu.SemaphoreType.DMA((1,)),
            pltpu.SemaphoreType.DMA((tensor_count,)),
        ],
        compiler_params=vmem_limit(28),
        cost_estimate=pl.CostEstimate(
            flops=8 * rows * per_owner * rank * width,
            bytes_accessed=2 * per_owner * rank * width,
            transcendentals=0,
        ),
        name="lora",
    )(
        own,
        own_rows,
        pltpu.with_memory_space_constraint(others, pltpu.VMEM),
        pltpu.with_memory_space_constraint(others_rows, pltpu.VMEM),
        down_first,
        down_second,
        in_hbm(down),
        in_hbm(up),
    )
    terms = lax.all_to_all(outgoing, ("tensor", "pool"), split_axis=0, concat_axis=0, tiled=True)
    terms = terms.reshape(owners * rows, query_columns)

    flat_late, adapters, table, _ = lax.optimization_barrier(
        (flat_here, adapters, table, outgoing)
    )
    power = np.arange(head_width // 2, dtype=np.float64) * (-2.0 / head_width)
    freq = np.tile(ROPE_BASE**power, 2).astype(np.float32).reshape(1, head_width)
    projected, own_piece, cosine, sine, spread = pl.pallas_call(
        functools.partial(project_kernel, (steps, requests, capacity, per_owner)),
        out_shape=[
            in_vmem((count, query_columns), F32),
            in_vmem((count, head_width), BF),
            in_vmem((count, head_width), F32),
            in_vmem((count, head_width), F32),
            in_vmem((count, owners * rows), BF),
        ],
        in_specs=whole(*range(5)) + [anywhere] * 2,
        out_specs=whole(*range(5)),
        scratch_shapes=[
            pltpu.VMEM(query_weight.shape, BF),
            pltpu.VMEM(key_value_weight.shape, BF),
            pltpu.SemaphoreType.DMA((17,)),
        ],
        compiler_params=vmem_limit(28),
        cost_estimate=pl.CostEstimate(
            flops=2 * count * width * query_columns,
            bytes_accessed=2 * width * query_columns,
            transcendentals=0,
        ),
        name="project",
    )(
        flat_late,
        adapters,
        table,
        lengths.reshape(1, requests),
        jnp.asarray(freq),
        in_hbm(query_weight),
        in_hbm(key_value_weight),
    )

    dims = (steps, requests, heads, head_width)
    packed_rows = count * heads
    half_rows = packed_rows // 2
    sent, sent_second = pl.pallas_call(
        functools.partial(query_kernel, dims),
        out_shape=[
            jax.ShapeDtypeStruct((half_rows + count, head_width), BF),
            jax.ShapeDtypeStruct((half_rows, head_width), BF),
        ],
        in_specs=whole(*range(6)),
        out_specs=whole(*range(2)),
        scratch_shapes=[pltpu.VMEM((packed_rows, head_width), F32)],
        compiler_params=vmem_limit(8),
        name="query",
    )(terms, spread, projected, own_piece, cosine, sine)
    got = swapped(sent, "tensor", 0)
    got_second = swapped(sent_second, "tensor", 0)

    cache_here = pl.pallas_call(
        load_kernel,
        out_shape=in_vmem(cache.shape, BF),
        in_specs=[anywhere, pl.BlockSpec(memory_space=pl.ANY)],
        out_specs=whole(0)[0],
        scratch_shapes=[pltpu.SemaphoreType.DMA((1,))],
        compiler_params=vmem_limit(1),
        cost_estimate=pl.CostEstimate(
            flops=0, bytes_accessed=4 * cache.size, transcendentals=0
        ),
        name="load",
    )(in_hbm(cache), sent)

    lines = half_rows // 128
    attend_dims = (steps, requests, heads, head_width, kv_split)
    attend_scratch = [
        pltpu.VMEM((half_rows, context), F32),
        pltpu.VMEM((half_rows, count), F32),
        pltpu.VMEM((half_rows, context), BF),
        pltpu.VMEM((half_rows, count), BF),
        pltpu.VMEM((half_rows, head_width), F32),
    ]
    cost = pl.CostEstimate(
        flops=2 * packed_rows * context * head_width,
        bytes_accessed=cache.size,
        transcendentals=half_rows * context,
    )
    partials = []
    sending = None
    for half, other_query in enumerate((got, got_second)):
        sending = pl.pallas_call(
            functools.partial(send_kernel, attend_dims, half * (requests // 2)),
            out_shape=jax.ShapeDtypeStruct((half_rows + 4 * lines, head_width), BF),
            in_specs=[smem] + whole(*range(4)),
            out_specs=whole(0)[0],
            scratch_shapes=[pltpu.VMEM((lines, 128), F32)] + attend_scratch,
            compiler_params=vmem_limit(16),
            cost_estimate=cost,
            name="send",
        )(lengths, sent, got, other_query, cache_here)
        partials.append(swapped(sending, "tensor", 0))
    queries = lax.optimization_barrier((sent, sent_second, sending))
    merging = []
    for half in range(2):
        own, level = pl.pallas_call(
            functools.partial(own_kernel, attend_dims, half * (requests // 2)),
            out_shape=[
                jax.ShapeDtypeStruct((half_rows, head_width), F32),
                jax.ShapeDtypeStruct((lines, 128), F32),
            ],
            in_specs=[smem] + whole(*range(4)),
            out_specs=whole(*range(2)),
            scratch_shapes=attend_scratch,
            compiler_params=vmem_limit(16),
            cost_estimate=cost,
            name="own",
        )(lengths, sent, got, queries[half], cache_here)
        merging += [own, level, partials[half]]
    attended = pl.pallas_call(
        functools.partial(merge_kernel, dims),
        out_shape=jax.ShapeDtypeStruct((count, query_columns), BF),
        in_specs=whole(*range(6)),
        out_specs=whole(0)[0],
        scratch_shapes=[pltpu.VMEM((packed_rows, head_width), F32)],
        compiler_params=vmem_limit(8),
        name="merge",
    )(*merging)
    return attended.reshape(steps, requests, query_columns)


def solution(mesh):
    placed = (
        P(None, ("groups", "pool"), None),
        P(None, "tensor"),
        P(None, "tensor"),
        P(("groups", "pool"), "tensor", None, None, None),
        P(("groups", "pool")),
        P(("groups", "pool")),
        P("groups"),
        P(("groups", "tensor", "pool"), None, None),
        P(("groups", "tensor", "pool"), None, None),
    )
    return jax.shard_map(
        local,
        mesh=mesh,
        in_specs=placed,
        out_specs=P(None, ("groups", "pool"), "tensor"),
        check_vma=False,
    )
```

```python
import functools

import jax
import jax.numpy as jnp
import numpy as np
from jax import lax
from jax.experimental import pallas as pl
from jax.experimental.pallas import tpu as pltpu
from jax.sharding import PartitionSpec as P

ROPE_BASE = 500000.0
ADAPTER_SCALE = 0.5
MASKED = -1e30
BF = jnp.bfloat16
F32 = jnp.float32
I32 = jnp.int32


def swapped(value, axis, bit):
    mask = 2**bit
    pairs = [(source, source ^ mask) for source in range(lax.axis_size(axis))]
    return lax.ppermute(value, axis, pairs)


def iota(shape, axis):
    return lax.broadcasted_iota(I32, shape, axis)


def column_of(row):
    count = row.shape[1]
    eye = iota((count, count), 0) == iota((count, count), 1)
    return jnp.sum(jnp.where(eye, row, jnp.zeros_like(row)), axis=1, keepdims=True)


def row_of(column):
    count = column.shape[0]
    eye = iota((count, count), 0) == iota((count, count), 1)
    return jnp.sum(jnp.where(eye, column, jnp.zeros_like(column)), axis=0, keepdims=True)


def routes(adapters, table, per_owner):
    requests = adapters.shape[1]
    rows = table.shape[1]
    match = (iota((rows, requests), 0) == adapters).astype(F32)
    stored = jnp.dot(
        table.astype(F32), match, precision=lax.Precision.HIGHEST, preferred_element_type=F32
    ).astype(I32)
    owner = stored // per_owner
    local_row = stored - owner * per_owner
    owner_column = column_of(owner)
    ahead = iota((requests, requests), 0) < iota((requests, requests), 1)
    place = jnp.sum(
        jnp.where((owner_column == owner) & ahead, 1, 0), axis=0, keepdims=True
    )
    return owner, local_row, place


def picked(dims, pools, states_ref, adapters, table):
    steps, requests, capacity, per_owner, pool_count = dims
    owner, local_row, place = routes(adapters, table, per_owner)
    owner = jnp.concatenate([owner] * steps, axis=1)
    place = jnp.concatenate([place] * steps, axis=1)
    local_row = jnp.concatenate([local_row] * steps, axis=1)
    shape = (steps * capacity, steps * requests)
    row = iota(shape, 0)
    row_step = row // capacity
    slot = (place == row - row_step * capacity) & (row_step == iota(shape, 1) // requests)
    hits = [
        slot & (owner == lax.axis_index("tensor") * pool_count + pool) for pool in pools
    ]
    pick = jnp.concatenate([jnp.where(hit, 1.0, 0.0) for hit in hits], axis=0).astype(BF)
    states = jnp.dot(pick, states_ref[...], preferred_element_type=F32).astype(BF)
    rows = [jnp.sum(jnp.where(hit, local_row, 0), axis=1, keepdims=True) for hit in hits]
    return states, rows


def stage_kernel(dims, states_hbm, down_hbm, adapters_hbm, table_hbm, *rest):
    states, down, adapters, table, own, own_rows, other, other_rows, sem, other_sem = rest
    parts = sem.shape[0]
    size = down.shape[0] // parts
    first = [
        pltpu.make_async_copy(adapters_hbm, adapters, other_sem.at[1]),
        pltpu.make_async_copy(table_hbm, table, other_sem.at[2]),
        pltpu.make_async_copy(states_hbm, states, other_sem.at[0]),
    ]
    copies = []
    for part in range(parts):
        span = pl.ds(part * size, size)
        copies.append(pltpu.make_async_copy(down_hbm.at[span], down.at[span], sem.at[part]))
    for copy in first + copies:
        copy.start()
    for copy in first:
        copy.wait()
    pool = lax.axis_index("pool")
    chosen, rows = picked(dims, (pool, 1 - pool), states, adapters[...], table[...])
    count = own.shape[0]
    own[...] = chosen[:count]
    other[...] = chosen[count:]
    own_rows[...] = rows[0]
    other_rows[...] = rows[1]
    for copy in copies:
        copy.wait()


def more_kernel(first_row, down_hbm, after, down, sem):
    parts = sem.shape[0]
    size = down.shape[0] // parts
    copies = [
        pltpu.make_async_copy(
            down_hbm.at[pl.ds(first_row + part * size, size)],
            down.at[pl.ds(part * size, size)],
            sem.at[part],
        )
        for part in range(parts)
    ]
    for copy in copies:
        copy.start()
    for copy in copies:
        copy.wait()


def lora_kernel(
    dims,
    rank,
    own_ref,
    own_rows_ref,
    other_ref,
    other_rows_ref,
    down_first,
    down_second,
    down_hbm,
    up_hbm,
    out_ref,
    down_rest,
    up,
    low,
    down_sem,
    up_sem,
):
    steps, requests, capacity, per_owner, pool_count = dims
    rows = steps * capacity
    here_rows = down_first.shape[0] + down_second.shape[0]
    down_rows = down_rest.shape[0]
    up_parts = up_sem.shape[0]
    up_columns = up.shape[1] // up_parts
    rest_copy = pltpu.make_async_copy(
        down_hbm.at[pl.ds(here_rows, down_rows)], down_rest, down_sem.at[0]
    )

    def up_copy(part):
        columns = pl.ds(pl.multiple_of(part * up_columns, up_columns), up_columns)
        return pltpu.make_async_copy(
            up_hbm.at[:, columns], up.at[:, columns], up_sem.at[part]
        )

    rest_copy.start()

    @pl.loop(0, up_parts)
    def _(part):
        up_copy(part).start()

    pool = lax.axis_index("pool")
    local_rows = jnp.concatenate([own_rows_ref[...], other_rows_ref[...]], axis=0)
    states = jnp.concatenate([own_ref[...].astype(F32), other_ref[...].astype(F32)], axis=0).T.astype(BF)

    def factors_of(rows_ref, first_row):
        count = rows_ref.shape[0]
        piece = lax.dot_general(
            rows_ref[...], states, (((1,), (0,)), ((), ())), preferred_element_type=F32
        ).T
        holder = (iota(piece.shape, 1) + first_row) // rank
        low[:, pl.ds(first_row, count)] = jnp.where(
            holder == local_rows, piece.astype(BF), jnp.zeros(piece.shape, BF)
        )

    first_row = 0
    for staged in (down_first, down_second):
        for at in range(0, staged.shape[0], down_rows):
            factors_of(staged.at[pl.ds(at, down_rows)], first_row)
            first_row += down_rows

    @pl.loop(0, 1)
    def _(_):
        rest_copy.wait()

    factors_of(down_rest, here_rows)
    factors = low[...]
    for part in range(up_parts):
        up_copy(part).wait()
        columns = pl.ds(part * up_columns, up_columns)
        term = jnp.dot(factors, up[:, columns], preferred_element_type=F32).astype(BF)
        out_ref[part * pool_count + pool] = term[:rows]
        out_ref[part * pool_count + 1 - pool] = term[rows:]


def project_kernel(
    dims,
    states_ref,
    adapters_ref,
    table_ref,
    lengths_ref,
    freq_ref,
    weight_hbm,
    new_weight_hbm,
    out_ref,
    piece_ref,
    cosine_ref,
    sine_ref,
    spread_ref,
    weight,
    new_weight,
    sem,
):
    steps, requests, capacity, per_owner = dims
    parts = sem.shape[0] - 1
    depth = weight.shape[0] // parts
    new_copy = pltpu.make_async_copy(new_weight_hbm, new_weight, sem.at[parts])

    def part_copy(part):
        span = pl.ds(pl.multiple_of(part * depth, depth), depth)
        return pltpu.make_async_copy(weight_hbm.at[span], weight.at[span], sem.at[part])

    @pl.loop(0, parts)
    def _(part):
        part_copy(part).start()

    new_copy.start()

    rows = steps * capacity
    owner, _, place = routes(adapters_ref[...], table_ref[...], per_owner)
    owner = jnp.concatenate([column_of(owner)] * steps, axis=0)
    place = jnp.concatenate([column_of(place)] * steps, axis=0)
    shape = spread_ref.shape
    slot = iota(shape, 1)
    slot_owner = slot // rows
    slot_step = (slot - slot_owner * rows) // capacity
    slot_place = slot - slot_owner * rows - slot_step * capacity
    hit = (
        (slot_owner == owner)
        & (slot_place == place)
        & (slot_step == iota(shape, 0) // requests)
    )
    spread_ref[...] = jnp.where(hit, 1.0, 0.0).astype(BF)

    length = column_of(lengths_ref[...])
    position = jnp.concatenate([length + step for step in range(steps)], axis=0)
    angle = position.astype(F32) * freq_ref[...]
    cosine = jnp.cos(angle)
    sine = jnp.sin(angle)
    half = angle.shape[1] // 2
    sine = jnp.where(iota(angle.shape, 1) < half, -sine, sine)
    cosine_ref[...] = cosine
    sine_ref[...] = sine

    out_ref[...] = jnp.zeros_like(out_ref)

    @pl.loop(0, parts)
    def _(part):
        part_copy(part).wait()
        span = pl.ds(pl.multiple_of(part * depth, depth), depth)
        out_ref[...] += jnp.dot(
            states_ref[:, span], weight[span, :], preferred_element_type=F32
        )

    new_copy.wait()
    fresh = jnp.dot(states_ref[...], new_weight[...], preferred_element_type=F32)
    turned = fresh * cosine_ref[...] + pltpu.roll(fresh, half, 1) * sine_ref[...]
    is_first = lax.axis_index("tensor") % 2 == 0
    piece_ref[...] = jnp.where(is_first, turned, fresh).astype(BF)


def load_kernel(source, after, out_ref, sem):
    copy = pltpu.make_async_copy(source, out_ref, sem.at[0])
    copy.start()
    copy.wait()


def query_kernel(
    dims, terms_ref, spread_ref, projected_ref, cosine_ref, sine_ref, first_ref, second_ref, packed
):
    steps, requests, heads, head_width = dims
    correction = jnp.dot(spread_ref[...], terms_ref[...], preferred_element_type=F32)
    query = projected_ref[...] + ADAPTER_SCALE * correction
    cosine = cosine_ref[...]
    sine = sine_ref[...]
    count = packed.shape[0]
    for head in range(heads):
        vector = query[:, head * head_width : (head + 1) * head_width]
        vector = vector * cosine + pltpu.roll(vector, head_width // 2, 1) * sine
        for step in range(steps):
            packed[pl.ds(step * heads + head, requests, stride=steps * heads), :] = vector[
                step * requests : (step + 1) * requests
            ]
    half = count // 2
    first_ref[...] = packed[:half, :].astype(BF)
    second_ref[...] = packed[half:, :].astype(BF)


def attend(dims, first_request, lengths_ref, query_ref, cache_ref, keys, vals, scratch, store):
    steps, requests, heads, head_width, kv_split = dims
    scores_ref, recent_ref, weights_ref, new_weights_ref, acc_ref = scratch
    per_request = steps * heads
    mine = requests // 2
    count = mine * per_request
    scale = head_width ** (-0.5)
    context = cache_ref.shape[2]
    part = lax.axis_index("tensor") % kv_split
    base = part * context
    lane = iota((per_request, context), 1)
    for request in range(mine):
        span = pl.ds(request * per_request, per_request)
        score = lax.dot_general(
            query_ref[span, :],
            cache_ref[first_request + request, 0],
            (((1,), (1,)), ((), ())),
            preferred_element_type=F32,
        )
        scores_ref[span, :] = jnp.where(
            lane < lengths_ref[first_request + request] - base, score * scale, MASKED
        )
    rows = min(128, count)
    shape = (rows, steps * requests)
    column_step = iota(shape, 1) // requests
    column_request = iota(shape, 1) - column_step * requests
    row_request = iota(shape, 0) // per_request
    row_step = (iota(shape, 0) - row_request * per_request) // heads
    allowed = (column_step <= row_step) & (part == 0)
    ahead = column_request - row_request
    for at in range(count // rows):
        span = pl.ds(at * rows, rows)
        recent = lax.dot_general(
            query_ref[span, :], keys, (((1,), (1,)), ((), ())), preferred_element_type=F32
        )
        recent_ref[span, :] = jnp.where(
            allowed & (ahead == first_request + at * (rows // per_request)), recent * scale, MASKED
        )
    totals = []
    for at in range(count // rows):
        span = pl.ds(at * rows, rows)
        scores = scores_ref[span, :]
        recent = recent_ref[span, :]
        top = jnp.maximum(
            jnp.max(scores, axis=1, keepdims=True), jnp.max(recent, axis=1, keepdims=True)
        ) if scores.shape != recent.shape else jnp.max(
            jnp.maximum(scores, recent), axis=1, keepdims=True
        )
        e_cached = jnp.exp(scores - top)
        e_recent = jnp.exp(recent - top)
        total = (
            jnp.sum(e_cached, axis=1, keepdims=True) + jnp.sum(e_recent, axis=1, keepdims=True)
            if scores.shape != recent.shape
            else jnp.sum(e_cached + e_recent, axis=1, keepdims=True)
        )
        weights_ref[span, :] = e_cached.astype(BF)
        new_weights_ref[span, :] = e_recent.astype(BF)
        totals.append((top, total))
    for request in range(mine):
        span = pl.ds(request * per_request, per_request)
        acc_ref[span, :] = jnp.dot(
            weights_ref[span, :],
            cache_ref[first_request + request, 1],
            preferred_element_type=F32,
        )
    for at in range(count // rows):
        span = pl.ds(at * rows, rows)
        top, total = totals[at]
        acc = acc_ref[span, :] + jnp.dot(
            new_weights_ref[span, :], vals, preferred_element_type=F32
        )
        store(at, rows, acc * (1.0 / total), top + jnp.log(total))


def new_pieces(own, other):
    first = lax.axis_index("tensor") % 2 == 0
    keys = jnp.where(first, own.astype(F32), other.astype(F32)).astype(BF)
    vals = jnp.where(first, other.astype(F32), own.astype(F32)).astype(BF)
    return keys, vals


def own_kernel(
    dims, first, lengths_ref, sent_ref, got_ref, query_ref, cache_ref, out_ref, level_ref, *scratch
):
    keys, vals = new_pieces(sent_ref[...], got_ref[...])

    def store(at, rows, result, level):
        out_ref[pl.ds(at * rows, rows), :] = result
        for line in range(rows // 128):
            level_ref[pl.ds(at * (rows // 128) + line, 1), :] = row_of(
                level[line * 128 : (line + 1) * 128]
            )

    attend(dims, first, lengths_ref, query_ref, cache_ref, keys, vals, scratch, store)


def send_kernel(
    dims, first, lengths_ref, sent_ref, got_ref, query_ref, cache_ref, out_ref, levels, *scratch
):
    lines = levels.shape[0]
    count = lines * 128
    keys, vals = new_pieces(sent_ref[...], got_ref[...])

    def store(at, rows, result, level):
        out_ref[pl.ds(at * rows, rows), :] = result.astype(BF)
        for line in range(rows // 128):
            levels[pl.ds(at * (rows // 128) + line, 1), :] = row_of(
                level[line * 128 : (line + 1) * 128]
            )

    attend(dims, first, lengths_ref, query_ref, cache_ref, keys, vals, scratch, store)
    rest = levels[...]
    pieces = []
    for _ in range(3):
        piece = rest.astype(BF)
        pieces.append(piece)
        rest = rest - piece.astype(F32)
    pieces.append(jnp.zeros_like(pieces[0]))
    out_ref[pl.ds(count, 4 * lines), :] = jnp.concatenate(pieces, axis=0)


def merge_kernel(dims, *refs):
    steps, requests, heads, head_width = dims
    out_ref, packed = refs[6:]
    for half in range(2):
        own_ref, level_ref, got_ref = refs[3 * half : 3 * half + 3]
        count = own_ref.shape[0]
        lines = count // 128
        extra = got_ref[pl.ds(count, 4 * lines), :].astype(F32)
        theirs = extra[:lines] + extra[lines : 2 * lines] + extra[2 * lines : 3 * lines]
        mine = level_ref[...]
        top = jnp.maximum(mine, theirs)
        mine = jnp.exp(mine - top)
        theirs = jnp.exp(theirs - top)
        total = mine + theirs
        mine = mine / total
        theirs = theirs / total
        for line in range(lines):
            span = pl.ds(line * 128, 128)
            packed[pl.ds(half * count + line * 128, 128), :] = own_ref[span, :] * column_of(
                mine[line : line + 1]
            ) + got_ref[span, :].astype(F32) * column_of(theirs[line : line + 1])
    for step in range(steps):
        for head in range(heads):
            out_ref[
                step * requests : (step + 1) * requests,
                head * head_width : (head + 1) * head_width,
            ] = packed[pl.ds(step * heads + head, requests, stride=steps * heads), :].astype(BF)


def in_vmem(shape, dtype):
    return pltpu.VMEM(shape, dtype)


def in_hbm(value):
    return pltpu.with_memory_space_constraint(value, pltpu.HBM)


def vmem_limit(mebibytes):
    return pltpu.CompilerParams(vmem_limit_bytes=mebibytes * 2**20)


def whole(*refs):
    return [pl.BlockSpec(memory_space=pltpu.VMEM)] * len(refs)


def local(
    inputs,
    query_weight,
    key_value_weight,
    key_value_cache,
    lengths,
    request_adapter,
    adapter_storage_row,
    adapter_down_factors,
    adapter_up_factors,
):
    steps, requests, width = inputs.shape
    tensor_count = lax.axis_size("tensor")
    pool_count = lax.axis_size("pool")
    owners = tensor_count * pool_count
    head_width = key_value_cache.shape[-1]
    context = key_value_cache.shape[-2]
    kv_split = 2 * head_width // key_value_weight.shape[1]
    query_columns = query_weight.shape[1]
    heads = query_columns // head_width
    per_owner, rank, _ = adapter_down_factors.shape
    capacity = max(2, 2 * requests // owners)
    rows = steps * capacity
    count = steps * requests

    flat = inputs.reshape(count, width)
    adapters = request_adapter.reshape(1, requests)
    table = adapter_storage_row.reshape(1, -1)
    down = adapter_down_factors.reshape(per_owner * rank, width)
    up = adapter_up_factors.reshape(per_owner * rank, -1)
    cache = key_value_cache.reshape(requests, 2, context, head_width)
    anywhere = pl.BlockSpec(memory_space=pltpu.HBM)
    smem = pl.BlockSpec(memory_space=pltpu.SMEM)

    quarter = per_owner * rank // 4
    lora_dims = (steps, requests, capacity, per_owner, pool_count)
    flat_here, down_first, adapters, table, own, own_rows, others, others_rows = pl.pallas_call(
        functools.partial(stage_kernel, lora_dims),
        out_shape=[
            in_vmem(flat.shape, BF),
            in_vmem((2 * quarter, width), BF),
            in_vmem(adapters.shape, I32),
            in_vmem(table.shape, I32),
            in_vmem((rows, width), BF),
            in_vmem((rows, 1), I32),
            in_vmem((rows, width), BF),
            in_vmem((rows, 1), I32),
        ],
        in_specs=[anywhere] * 4,
        out_specs=whole(*range(8)),
        scratch_shapes=[pltpu.SemaphoreType.DMA((2,)), pltpu.SemaphoreType.DMA((3,))],
        compiler_params=vmem_limit(8),
        name="stage",
    )(in_hbm(flat), in_hbm(down), in_hbm(adapters), in_hbm(table))
    others = swapped(others, "pool", 0)
    others_rows = swapped(others_rows, "pool", 0)

    down_second = pl.pallas_call(
        functools.partial(more_kernel, 2 * quarter),
        out_shape=in_vmem((quarter, width), BF),
        in_specs=[anywhere, pl.BlockSpec(memory_space=pl.ANY)],
        out_specs=whole(0)[0],
        scratch_shapes=[pltpu.SemaphoreType.DMA((4,))],
        compiler_params=vmem_limit(1),
        cost_estimate=pl.CostEstimate(flops=0, bytes_accessed=2 * down.size, transcendentals=0),
        name="more",
    )(in_hbm(down), own_rows)

    outgoing = pl.pallas_call(
        functools.partial(lora_kernel, lora_dims, rank),
        out_shape=jax.ShapeDtypeStruct((owners, rows, query_columns), BF),
        in_specs=whole(*range(6)) + [anywhere] * 2,
        out_specs=whole(0)[0],
        scratch_shapes=[
            pltpu.VMEM((quarter, width), BF),
            pltpu.VMEM(up.shape, BF),
            pltpu.VMEM((2 * rows, per_owner * rank), BF),
            pltpu.SemaphoreType.DMA((1,)),
            pltpu.SemaphoreType.DMA((tensor_count,)),
        ],
        compiler_params=vmem_limit(28),
        cost_estimate=pl.CostEstimate(
            flops=8 * rows * per_owner * rank * width,
            bytes_accessed=2 * per_owner * rank * width,
            transcendentals=0,
        ),
        name="lora",
    )(
        own,
        own_rows,
        pltpu.with_memory_space_constraint(others, pltpu.VMEM),
        pltpu.with_memory_space_constraint(others_rows, pltpu.VMEM),
        down_first,
        down_second,
        in_hbm(down),
        in_hbm(up),
    )
    terms = lax.all_to_all(outgoing, ("tensor", "pool"), split_axis=0, concat_axis=0, tiled=True)
    terms = terms.reshape(owners * rows, query_columns)

    flat_late, adapters, table, _ = lax.optimization_barrier(
        (flat_here, adapters, table, outgoing)
    )
    power = np.arange(head_width // 2, dtype=np.float64) * (-2.0 / head_width)
    freq = np.tile(ROPE_BASE**power, 2).astype(np.float32).reshape(1, head_width)
    projected, own_piece, cosine, sine, spread = pl.pallas_call(
        functools.partial(project_kernel, (steps, requests, capacity, per_owner)),
        out_shape=[
            in_vmem((count, query_columns), F32),
            in_vmem((count, head_width), BF),
            in_vmem((count, head_width), F32),
            in_vmem((count, head_width), F32),
            in_vmem((count, owners * rows), BF),
        ],
        in_specs=whole(*range(5)) + [anywhere] * 2,
        out_specs=whole(*range(5)),
        scratch_shapes=[
            pltpu.VMEM(query_weight.shape, BF),
            pltpu.VMEM(key_value_weight.shape, BF),
            pltpu.SemaphoreType.DMA((17,)),
        ],
        compiler_params=vmem_limit(28),
        cost_estimate=pl.CostEstimate(
            flops=2 * count * width * query_columns,
            bytes_accessed=2 * width * query_columns,
            transcendentals=0,
        ),
        name="project",
    )(
        flat_late,
        adapters,
        table,
        lengths.reshape(1, requests),
        jnp.asarray(freq),
        in_hbm(query_weight),
        in_hbm(key_value_weight),
    )

    other_piece = swapped(own_piece, "tensor", 0)
    spread, other_piece = lax.optimization_barrier((spread, other_piece))
    dims = (steps, requests, heads, head_width)
    packed_rows = count * heads
    half_rows = packed_rows // 2
    sent, sent_second = pl.pallas_call(
        functools.partial(query_kernel, dims),
        out_shape=[
            jax.ShapeDtypeStruct((half_rows, head_width), BF),
            jax.ShapeDtypeStruct((half_rows, head_width), BF),
        ],
        in_specs=whole(*range(5)),
        out_specs=whole(*range(2)),
        scratch_shapes=[pltpu.VMEM((packed_rows, head_width), F32)],
        compiler_params=vmem_limit(8),
        name="query",
    )(terms, spread, projected, cosine, sine)
    got = swapped(sent, "tensor", 0)
    got_second = swapped(sent_second, "tensor", 0)

    cache_here = pl.pallas_call(
        load_kernel,
        out_shape=in_vmem(cache.shape, BF),
        in_specs=[anywhere, pl.BlockSpec(memory_space=pl.ANY)],
        out_specs=whole(0)[0],
        scratch_shapes=[pltpu.SemaphoreType.DMA((1,))],
        compiler_params=vmem_limit(1),
        cost_estimate=pl.CostEstimate(
            flops=0, bytes_accessed=4 * cache.size, transcendentals=0
        ),
        name="load",
    )(in_hbm(cache), sent)

    lines = half_rows // 128
    attend_dims = (steps, requests, heads, head_width, kv_split)
    attend_scratch = [
        pltpu.VMEM((half_rows, context), F32),
        pltpu.VMEM((half_rows, count), F32),
        pltpu.VMEM((half_rows, context), BF),
        pltpu.VMEM((half_rows, count), BF),
        pltpu.VMEM((half_rows, head_width), F32),
    ]
    cost = pl.CostEstimate(
        flops=2 * packed_rows * context * head_width,
        bytes_accessed=cache.size,
        transcendentals=half_rows * context,
    )
    partials = []
    sending = None
    for half, other_query in enumerate((got, got_second)):
        sending = pl.pallas_call(
            functools.partial(send_kernel, attend_dims, half * (requests // 2)),
            out_shape=jax.ShapeDtypeStruct((half_rows + 4 * lines, head_width), BF),
            in_specs=[smem] + whole(*range(4)),
            out_specs=whole(0)[0],
            scratch_shapes=[pltpu.VMEM((lines, 128), F32)] + attend_scratch,
            compiler_params=vmem_limit(16),
            cost_estimate=cost,
            name="send",
        )(lengths, own_piece, other_piece, other_query, cache_here)
        partials.append(swapped(sending, "tensor", 0))
    queries = lax.optimization_barrier((sent, sent_second, sending))
    merging = []
    for half in range(2):
        own, level = pl.pallas_call(
            functools.partial(own_kernel, attend_dims, half * (requests // 2)),
            out_shape=[
                jax.ShapeDtypeStruct((half_rows, head_width), F32),
                jax.ShapeDtypeStruct((lines, 128), F32),
            ],
            in_specs=[smem] + whole(*range(4)),
            out_specs=whole(*range(2)),
            scratch_shapes=attend_scratch,
            compiler_params=vmem_limit(16),
            cost_estimate=cost,
            name="own",
        )(lengths, own_piece, other_piece, queries[half], cache_here)
        merging += [own, level, partials[half]]
    attended = pl.pallas_call(
        functools.partial(merge_kernel, dims),
        out_shape=jax.ShapeDtypeStruct((count, query_columns), BF),
        in_specs=whole(*range(6)),
        out_specs=whole(0)[0],
        scratch_shapes=[pltpu.VMEM((packed_rows, head_width), F32)],
        compiler_params=vmem_limit(8),
        name="merge",
    )(*merging)
    return attended.reshape(steps, requests, query_columns)


def solution(mesh):
    placed = (
        P(None, ("groups", "pool"), None),
        P(None, "tensor"),
        P(None, "tensor"),
        P(("groups", "pool"), "tensor", None, None, None),
        P(("groups", "pool")),
        P(("groups", "pool")),
        P("groups"),
        P(("groups", "tensor", "pool"), None, None),
        P(("groups", "tensor", "pool"), None, None),
    )
    return jax.shard_map(
        local,
        mesh=mesh,
        in_specs=placed,
        out_specs=P(None, ("groups", "pool"), "tensor"),
        check_vma=False,
    )
```
